128 devices in a mesh: gx: 8 (over y, x_lo), gy: 16 (over z, x_hi, core).
Axes of the slice: x: 4 (x_hi: 2, x_lo: 2; x = x_hi * 2 + x_lo), y: 4, z: 4, core: 2. Of those that a mesh axis runs over, the one named last changes fastest.
Arguments:
- positions: float32 [8, 16, 3, 256], P('gx', 'gy'), may hold values from 0 to 1
- species: int32 [8, 16, 256], P('gx', 'gy'), may hold values from 0 to 88
- dest_key: int32 [8, 16, 256], P('gx', 'gy'), may hold values from 0 to 4, as said below
- send_list: int32 [8, 16, 4, 32], P('gx', 'gy'), may hold values from 0 to 255, as said below
- send_count: int32 [8, 16, 4], P('gx', 'gy'), may hold values from 8 to 32, as said below
- border: int32 [8, 16, 128], P('gx', 'gy'), may hold values from 0 to 255, as said below
- neighbours: int32 [8, 16, 384, 12], P('gx', 'gy'), may hold values from -1 to 1535, as said below
- embedding: float32 [89, 128], replicated, may hold values from -4 to 4
- radial_in: float32 [2, 8, 64], replicated, may hold values from -2 to 2
- radial_mid: float32 [2, 64, 64], replicated, may hold values from -0.75 to 0.75
- radial_out_one: float32 [64, 384], replicated, may hold values from -4 to 4
- radial_out_two: float32 [64, 896], replicated, may hold values from -4 to 4
- mix: float32 [2, 3, 128, 128], replicated, may hold values from -0.5 to 0.5
- mix_out_one: float32 [3, 128, 128], replicated, may hold values from -0.5 to 0.5
- mix_out_two: float32 [128, 128], replicated, may hold values from -0.5 to 0.5
- product_one: float32 [5, 128], replicated, may hold values from -4 to 4
- product_two: float32 [3, 128], replicated, may hold values from -4 to 4
- read_lin: float32 [128], replicated, may hold values from -0.5 to 0.5
- read_hidden: float32 [128, 16], replicated, may hold values from -0.5 to 0.5
- read_out: float32 [16], replicated, may hold values from -1.5 to 1.5
Outputs:
- atom_energy: float32 [8, 16, 384], P('gx', 'gy')
- forces: float32 [8, 16, 3, 384], P('gx', 'gy')
The draws below stay inside these ranges and needn't reach their ends.
Inputs may be any that keep to these rules, and one draw needn't show every extreme that they name: `dest_key`: 0 keeps the atom; 1, 2, 3, 4 send it to the next device along gx, the previous along gx, the next along gy, the previous along gy (periodic); each device has at most 32 atoms of each nonzero key. `send_list`: row d holds in increasing order the slots whose dest_key is d + 1, then other slots as padding. `send_count`: the number of slots whose dest_key is d + 1; some device has exactly 32 in some direction in every draw. `border`: distinct slots whose dest_key is 0. `neighbours`: -1 marks an empty slot; a value below 384 is a local row after migration; 384 + (3 * a + b) * 128 + k is the k-th border row of the device at offset (a - 1, b - 1) along (gx, gy), with (a, b) never (1, 1); devices differ in how many slots are empty.
All inputs are finite; a program needn't handle non-finite values.
Results may differ from the reference program's by a relative error of at most 0.003.
Values may be sent and summed in bfloat16 or wider, within the bound.
No kernel may reach another device: no remote copies, remote signals or barrier semaphores. Data moves between devices by JAX's collectives and lax.ppermute only.
A program may use at most 192 MiB of HBM per device.

```python
import math
import jax
import jax.numpy as jnp
from jax import lax

C = 128
H = 64
NB = 8
NELEM = 89
RH = 16
K = 12
M = 32
B = 128
A_OWN = 256
R = 384
GRID_X = 8
GRID_Y = 16
N_GX = 8
N_GY = 16


def migration_plan(key):
    device_total = GRID_X * GRID_Y
    count_key, hot_key, order_key = jax.random.split(key, 3)
    counts = jax.random.randint(count_key, (device_total * 4,), M // 4, M + 1)
    hottest = jax.random.randint(hot_key, (), 0, device_total * 4)
    counts = jnp.where(jnp.arange(device_total * 4) == hottest, M, counts).reshape(device_total, 4).astype(jnp.int32)
    orders = jax.vmap(lambda sub_key: jax.random.permutation(sub_key, A_OWN))(jax.random.split(order_key, device_total))
    limits = jnp.cumsum(counts, axis=1)
    places = jnp.arange(A_OWN)
    passed = jnp.sum((places[None, None, :] >= limits[:, :, None]).astype(jnp.int32), axis=1)
    label_at = jnp.where(places[None, :] < limits[:, 3:4], passed + 1, 0).astype(jnp.int32)
    labels = jax.vmap(lambda order, label: jnp.zeros((A_OWN,), jnp.int32).at[order].set(label))(orders, label_at)
    listed = jnp.stack([jnp.argsort((labels != target + 1).astype(jnp.int32), axis=1, stable=True)[:, :M] for target in range(4)], axis=1).astype(jnp.int32)
    border_rows = orders[:, A_OWN - B:].astype(jnp.int32)
    return (labels, listed, counts, border_rows)


def draw_dest_key(key, part):
    labels, listed, counts, border_rows = migration_plan(key)
    return labels.reshape(GRID_X, GRID_Y, A_OWN)


def draw_send_list(key, part):
    labels, listed, counts, border_rows = migration_plan(key)
    return listed.reshape(GRID_X, GRID_Y, 4, M)


def draw_send_count(key, part):
    labels, listed, counts, border_rows = migration_plan(key)
    return counts.reshape(GRID_X, GRID_Y, 4)


def draw_border(key, part):
    labels, listed, counts, border_rows = migration_plan(key)
    return border_rows.reshape(GRID_X, GRID_Y, B)


def draw_neighbours(key, part):
    key = jax.random.fold_in(key, 7)
    device_total = GRID_X * GRID_Y
    level_key, valid_key, ghost_key, block_key, inner_key, local_key = jax.random.split(key, 6)
    levels = jax.random.randint(level_key, (device_total, 1, 1), 2, 9)
    valid = jax.random.randint(valid_key, (device_total, R, K), 0, 8) < levels
    ghostly = jax.random.randint(ghost_key, (device_total, R, K), 0, 3) > 0
    blocks = jax.random.randint(block_key, (device_total, R, K), 0, 8)
    blocks = blocks + (blocks >= 4).astype(jnp.int32)
    ghost_index = R + blocks * B + jax.random.randint(inner_key, (device_total, R, K), 0, B)
    local_index = jax.random.randint(local_key, (device_total, R, K), 0, R)
    chosen = jnp.where(valid, jnp.where(ghostly, ghost_index, local_index), -1).astype(jnp.int32)
    chosen = chosen.at[0, 0, 0].set(R + 9 * B - 1)
    return chosen.reshape(GRID_X, GRID_Y, R, K)


def plant(result, key, low, largest):
    longest = result.shape.index(max(result.shape))
    spots = []
    for shift in (0, 1):
        where = [jax.random.randint(jax.random.fold_in(key, axis), (), 0, length) for axis, length in enumerate(result.shape)]
        where[longest] = (where[longest] + shift) % result.shape[longest]
        spots.append(tuple(where))
    return result.at[spots[0]].set(low).at[spots[1]].set(largest)


def level_of(key, shape, shards, smallest, high):
    factor_of = 1.0
    for dim, parts in shards:
        draws = jax.random.uniform(jax.random.fold_in(jax.random.fold_in(key, 6), dim), (parts,), jnp.float32, smallest / len(shards), high / len(shards))
        factor_of = factor_of * jnp.repeat(jnp.exp(draws), shape[dim] // parts).reshape((-1,) + (1,) * (len(shape) - 1 - dim))
    return factor_of


def gaussian(own_key, shape, deviation, reach, kind=jnp.bfloat16):
    return jnp.clip(deviation * jax.random.normal(own_key, shape, jnp.float32), -reach, reach).astype(kind)


def setup_inputs(seed: int = 0) -> dict:
    splits = jax.random.split(jax.random.key(seed), 21)
    return {
        "positions": jnp.clip(1.0 * jax.random.uniform(splits[0], (GRID_X, GRID_Y, 3, A_OWN), jnp.float32) ** level_of(splits[0], (GRID_X, GRID_Y, 3, A_OWN), ((0, 8), (1, 16)), -0.2, 0.2), 0.0, 1.0),
        "species": plant(jax.random.randint(splits[1], (GRID_X, GRID_Y, A_OWN), 0, NELEM), jax.random.fold_in(splits[1], 1), 0, NELEM - 1).astype(jnp.int32),
        "dest_key": draw_dest_key(jax.random.fold_in(splits[20], 71), 0),
        "send_list": draw_send_list(jax.random.fold_in(splits[20], 71), 0),
        "send_count": draw_send_count(jax.random.fold_in(splits[20], 71), 0),
        "border": draw_border(jax.random.fold_in(splits[20], 71), 0),
        "neighbours": draw_neighbours(jax.random.fold_in(splits[20], 71), 0),
        "embedding": gaussian(splits[7], (NELEM, C), 1.0, 4.0, jnp.float32),
        "radial_in": gaussian(splits[8], (2, NB, H), NB ** -0.5, 2.0, jnp.float32),
        "radial_mid": gaussian(splits[9], (2, H, H), H ** -0.5, 0.75, jnp.float32),
        "radial_out_one": gaussian(splits[10], (H, 3 * C), 1.0, 4.0, jnp.float32),
        "radial_out_two": gaussian(splits[11], (H, 7 * C), 1.0, 4.0, jnp.float32),
        "mix": gaussian(splits[12], (2, 3, C, C), C ** -0.5, 0.5, jnp.float32),
        "mix_out_one": gaussian(splits[13], (3, C, C), C ** -0.5, 0.5, jnp.float32),
        "mix_out_two": gaussian(splits[14], (C, C), C ** -0.5, 0.5, jnp.float32),
        "product_one": gaussian(splits[15], (5, C), 1.0, 4.0, jnp.float32),
        "product_two": gaussian(splits[16], (3, C), 1.0, 4.0, jnp.float32),
        "read_lin": gaussian(splits[17], (C,), C ** -0.5, 0.5, jnp.float32),
        "read_hidden": gaussian(splits[18], (C, RH), C ** -0.5, 0.5, jnp.float32),
        "read_out": gaussian(splits[19], (RH,), RH ** -0.5, 1.5, jnp.float32),
    }


cutoff_radius = 5.0
cell_side = 1.0
highest = lax.Precision.HIGHEST

def geometry(offsets, basis_count):
    squared = lax.optimization_barrier(jnp.sum(offsets * offsets, axis=0)) + 1.0
    distance = jnp.sqrt(squared)
    pointer = offsets / distance[None, :]
    scaled = distance / cutoff_radius
    sixth = scaled * scaled * scaled * scaled * scaled * scaled
    envelope = 1.0 - 28.0 * sixth + 48.0 * sixth * scaled - 21.0 * sixth * scaled * scaled
    orders = jnp.arange(1, basis_count + 1).astype(jnp.float32)[:, None]
    basis = math.sqrt(2.0 / cutoff_radius) * jnp.sin(orders * (math.pi / cutoff_radius) * distance[None, :]) * (envelope / distance)[None, :]
    along_x = pointer[0]
    along_y = pointer[1]
    along_z = pointer[2]
    root_five = math.sqrt(5.0)
    root_fifteen = math.sqrt(15.0)
    vector_part = math.sqrt(3.0) * pointer
    tensor_part = jnp.stack([root_fifteen * along_x * along_y, root_fifteen * along_y * along_z, 0.5 * root_five * (2.0 * along_z * along_z - along_x * along_x - along_y * along_y), root_fifteen * along_x * along_z, 0.5 * root_fifteen * (along_x * along_x - along_y * along_y)])
    return (basis, vector_part, tensor_part)

def radial(basis, w_in, w_mid, w_out):
    hidden = jax.nn.silu(jnp.dot(w_in.T, basis, precision=highest))
    hidden = jax.nn.silu(jnp.dot(w_mid.T, hidden, precision=highest))
    return jnp.dot(w_out.T, hidden, precision=highest)

def contract(matrix, values):
    return jnp.einsum('cd,...cn->...dn', matrix, values, precision=highest)

def interaction(first, pos_all, feats_all, occ_all, neighbour_block, pos_block, occ_block, residual, weights):
    w_in, w_mid, w_out, mixing, mixing_out, coefs = weights
    atoms, slots = neighbour_block.shape
    channels = mixing.shape[-1]
    flat_index = jnp.maximum(neighbour_block, 0).reshape(-1)
    edge_mask = (neighbour_block >= 0).astype(jnp.float32).reshape(-1) * occ_all[flat_index] * jnp.repeat(occ_block, slots)
    offsets = pos_all[:, flat_index] - jnp.repeat(pos_block, slots, axis=1)
    basis, vector_part, tensor_part = geometry(offsets, w_in.shape[0])
    source = feats_all[:, flat_index] * edge_mask[None, :]
    paths = 3 if first else 7
    edge_weights = radial(basis, w_in, w_mid, w_out).reshape(paths, channels, -1)
    scalar = source[:channels]
    if first:
        msg_scalar = edge_weights[0] * scalar
        msg_vector = edge_weights[1][None] * scalar[None] * vector_part[:, None]
        msg_tensor = edge_weights[2][None] * scalar[None] * tensor_part[:, None]
    else:
        vectors = source[channels:4 * channels].reshape(3, channels, -1)
        tensors = source[4 * channels:].reshape(5, channels, -1)
        msg_scalar = edge_weights[0] * scalar + edge_weights[1] * lax.optimization_barrier(jnp.sum(vector_part[:, None] * vectors, axis=0)) + edge_weights[2] * lax.optimization_barrier(jnp.sum(tensor_part[:, None] * tensors, axis=0))
        msg_vector = edge_weights[3][None] * scalar[None] * vector_part[:, None] + edge_weights[4][None] * vectors
        msg_tensor = edge_weights[5][None] * scalar[None] * tensor_part[:, None] + edge_weights[6][None] * tensors

    def pooling(message):
        return lax.optimization_barrier(jnp.sum(message.reshape(message.shape[:-1] + (atoms, slots)), axis=-1)) / slots
    mixed_scalar = contract(mixing[0], pooling(msg_scalar))
    mixed_vector = contract(mixing[1], pooling(msg_vector))
    mixed_tensor = contract(mixing[2], pooling(msg_tensor))
    product_scalar = mixed_scalar + coefs[0][:, None] * mixed_scalar * mixed_scalar + coefs[1][:, None] * lax.optimization_barrier(jnp.sum(mixed_vector * mixed_vector, axis=0)) + coefs[2][:, None] * lax.optimization_barrier(jnp.sum(mixed_tensor * mixed_tensor, axis=0))
    if first:
        product_vector = mixed_vector * (1.0 + coefs[3][:, None] * mixed_scalar)[None]
        product_tensor = mixed_tensor * (1.0 + coefs[4][:, None] * mixed_scalar)[None]
        new_scalar = contract(mixing_out[0], product_scalar) + residual
        new_vector = contract(mixing_out[1], product_vector).reshape(3 * channels, atoms)
        new_tensor = contract(mixing_out[2], product_tensor).reshape(5 * channels, atoms)
        return jnp.concatenate([new_scalar, new_vector, new_tensor], axis=0)
    return contract(mixing_out, product_scalar) + residual[:channels]

def run_layer(first, pos_all, feats_all, occ_all, occupied, neighbour_rows, weights):
    total_rows = neighbour_rows.shape[0]
    block_rows = math.gcd(total_rows, 128)
    block_count = total_rows // block_rows

    def one_block(block_index):
        start = block_index * block_rows
        neighbour_block = lax.dynamic_slice_in_dim(neighbour_rows, start, block_rows, 0)
        pos_block = lax.dynamic_slice_in_dim(pos_all, start, block_rows, 1)
        occ_block = lax.dynamic_slice_in_dim(occupied, start, block_rows, 0)
        residual = lax.dynamic_slice_in_dim(feats_all, start, block_rows, 1)
        return interaction(first, pos_all, feats_all, occ_all, neighbour_block, pos_block, occ_block, residual, weights)
    outputs = lax.map(jax.checkpoint(one_block), jnp.arange(block_count, dtype=jnp.int32))
    return jnp.moveaxis(outputs, 0, 1).reshape(outputs.shape[1], total_rows)

def shift_table():
    grid_shift = cell_side * (jnp.arange(3).astype(jnp.float32) - 1.0)
    first_axis = jnp.broadcast_to(grid_shift[:, None], (3, 3))
    second_axis = jnp.broadcast_to(grid_shift[None, :], (3, 3))
    return jnp.stack([first_axis, second_axis, jnp.zeros((3, 3), jnp.float32)], axis=-1)

def surround(table, grid_row, grid_column):
    blocks = []
    for across in range(3):
        line = []
        for alongside in range(3):
            line.append(table[(grid_row + across - 1) % N_GX, (grid_column + alongside - 1) % N_GY])
        blocks.append(jnp.stack(line))
    return jnp.stack(blocks)

def migrate(positions, species, dest_key, send_list, send_count):
    picked = jax.vmap(jax.vmap(lambda coords_row, listed: coords_row[:, listed]))(positions, send_list)
    picked_kinds = jax.vmap(jax.vmap(lambda kinds_row, listed: kinds_row[listed]))(species, send_list)
    slot_used = jnp.arange(send_list.shape[-1])[None, None, None, :] < send_count[..., None]
    picked_kinds = jnp.where(slot_used, picked_kinds, -1)
    arrival_moves = ((1, 0, 0), (-1, 0, 0), (1, 1, 1), (-1, 1, 1))
    coords_parts = [positions]
    kinds_parts = [species]
    occupied_parts = [(dest_key == 0).astype(jnp.float32)]
    for target in range(4):
        amount, grid_axis, coordinate = arrival_moves[target]
        moved = jnp.roll(picked[:, :, :, target], amount, axis=grid_axis)
        moved = moved.at[:, :, coordinate].add(-amount * cell_side)
        moved_kinds = jnp.roll(picked_kinds[:, :, target], amount, axis=grid_axis)
        coords_parts.append(moved)
        kinds_parts.append(moved_kinds)
        occupied_parts.append((moved_kinds >= 0).astype(jnp.float32))
    return (jnp.concatenate(coords_parts, axis=3), jnp.concatenate(kinds_parts, axis=2), jnp.concatenate(occupied_parts, axis=2))

def reference(positions, species, dest_key, send_list, send_count, border, neighbours, embedding, radial_in, radial_mid, radial_out_one, radial_out_two, mix, mix_out_one, mix_out_two, product_one, product_two, read_lin, read_hidden, read_out):
    coords, kinds, occupied = migrate(positions, species, dest_key, send_list, send_count)
    channels = embedding.shape[1]
    border_count = border.shape[-1]
    border_kinds = jax.vmap(jax.vmap(lambda kinds_row, rows_picked: kinds_row[rows_picked]))(kinds, border)
    first_weights = (radial_in[0], radial_mid[0], radial_out_one, mix[0], mix_out_one, product_one)
    second_weights = (radial_in[1], radial_mid[1], radial_out_two, mix[1], mix_out_two, product_two)
    offsets_grid = shift_table()
    device_total = N_GX * N_GY

    def total_energy(coords_in):
        border_coords = jax.vmap(jax.vmap(lambda coords_row, rows_picked: coords_row[:, rows_picked]))(coords_in, border)

        def assemble(device_index):
            grid_row = device_index // N_GY
            grid_column = device_index % N_GY
            beside_all = surround(border_coords, grid_row, grid_column) + offsets_grid[:, :, :, None]
            ghost = jnp.moveaxis(beside_all, 2, 0).reshape(3, 9 * border_count)
            pos_all = jnp.concatenate([coords_in[grid_row, grid_column], ghost], axis=1)
            occ_local = occupied[grid_row, grid_column]
            occ_all = jnp.concatenate([occ_local, jnp.ones((9 * border_count,), jnp.float32)])
            return (grid_row, grid_column, pos_all, occ_local, occ_all)

        def layer_one_device(device_index):
            grid_row, grid_column, pos_all, occ_local, occ_all = assemble(device_index)
            ghost_kinds = surround(border_kinds, grid_row, grid_column).reshape(9 * border_count)
            kinds_all = jnp.maximum(jnp.concatenate([kinds[grid_row, grid_column], ghost_kinds]), 0)
            initial = embedding[kinds_all].T
            return run_layer(True, pos_all, initial, occ_all, occ_local, neighbours[grid_row, grid_column], first_weights)
        hidden_all = lax.map(jax.checkpoint(layer_one_device), jnp.arange(device_total, dtype=jnp.int32))
        rounded = lax.optimization_barrier(hidden_all.astype(jnp.bfloat16)).astype(jnp.float32)
        hidden_used = hidden_all + lax.stop_gradient(rounded - hidden_all)
        hidden_grid = hidden_used.reshape((N_GX, N_GY) + hidden_used.shape[1:])
        border_feats = jax.vmap(jax.vmap(lambda feats_row, rows_picked: feats_row[:, rows_picked]))(hidden_grid, border)

        def layer_two_device(device_index):
            grid_row, grid_column, pos_all, occ_local, occ_all = assemble(device_index)
            beside_all = surround(border_feats, grid_row, grid_column)
            ghost = jnp.moveaxis(beside_all, 2, 0).reshape(beside_all.shape[2], 9 * border_count)
            table = jnp.concatenate([hidden_grid[grid_row, grid_column], ghost], axis=1)
            scalars = run_layer(False, pos_all, table, occ_all, occ_local, neighbours[grid_row, grid_column], second_weights)
            readout = jax.nn.silu(jnp.dot(read_hidden.T, scalars, precision=highest))
            return occ_local * jnp.dot(read_out, readout, precision=highest)
        energy_two = lax.map(jax.checkpoint(layer_two_device), jnp.arange(device_total, dtype=jnp.int32))
        energy_two = energy_two.reshape(N_GX, N_GY, -1)
        energy_one = occupied * jnp.einsum('c,xycr->xyr', read_lin, hidden_grid[:, :, :channels], precision=highest)
        atom_energy = energy_one + energy_two
        return (jnp.sum(atom_energy), atom_energy)
    (total_value, atom_energy), gradient = jax.value_and_grad(total_energy, has_aux=True)(coords)
    return (atom_energy, -gradient)
```

```python
import functools
import math

import jax
import jax.numpy as jnp
from jax import lax
from jax.experimental import pallas as pl
from jax.experimental.pallas import tpu as pltpu
from jax.sharding import PartitionSpec as P

f32 = jnp.float32
bf16 = jnp.bfloat16
CH = 128
HID = 64
SLOTS = 12
LANES = 128
EDGES = SLOTS * LANES
LOCAL = 3
COLS = 11 * LANES
RADIUS = 5.0
SCALE = math.sqrt(2.0 / RADIUS)
R3 = math.sqrt(3.0)
R5 = math.sqrt(5.0)
R15 = math.sqrt(15.0)
VMEM = pl.BlockSpec(memory_space=pltpu.VMEM)
SMEM = pl.BlockSpec(memory_space=pltpu.SMEM)
LIMIT = 60 * 1024 * 1024


def call(kernel, out_shape, scratch=(), flops=1000000, in_specs=None, **kw):
    return pl.pallas_call(
        kernel,
        out_shape=out_shape,
        scratch_shapes=list(scratch),
        compiler_params=pltpu.CompilerParams(vmem_limit_bytes=LIMIT),
        cost_estimate=pl.CostEstimate(flops=flops, bytes_accessed=1000000, transcendentals=0),
        **({"in_specs": in_specs} if in_specs is not None else {}),
        **kw,
    )


def shape(*dims, kind=f32):
    return jax.ShapeDtypeStruct(dims, kind)


def lanes(i, n=1):
    return slice(i * LANES, (i + n) * LANES)


def hi_lo(x):
    hi = x.astype(bf16)
    return hi, (x - hi.astype(f32)).astype(bf16)


def split3(x):
    hi, lo = hi_lo(x)
    return jnp.concatenate([hi, lo, hi], axis=0)


def mm(a, b):
    return jnp.dot(a, b, preferred_element_type=f32)


def mm_nt(a, b):
    return lax.dot_general(a, b, (((1,), (1,)), ((), ())), preferred_element_type=f32)


def silu_parts(x):
    s = 0.5 * jnp.tanh(0.5 * x) + 0.5
    h = x * s
    return h, s + h * (1.0 - s)


def take_lanes(chunk, index):
    return jnp.take_along_axis(chunk, index, axis=1, mode="promise_in_bounds")


def gather_columns(ref, rows, index, chunks):
    low = index & 127
    block = index >> 7
    out = take_lanes(ref[rows, lanes(0)], low)
    for c in range(1, chunks):
        out = jnp.where(block == c, take_lanes(ref[rows, lanes(c)], low), out)
    return out


def packet_kernel(pos, spec, listed, border, count, out, tbl):
    tbl[...] = jnp.zeros_like(tbl)
    tbl[0:3, :] = pos[...]
    tbl[3:4, :] = spec[...].astype(f32)
    row = lax.broadcasted_iota(jnp.int32, (8, LANES), 0)
    lane = lax.broadcasted_iota(jnp.int32, (8, LANES), 1)
    way = lane >> 5
    index = jnp.broadcast_to(listed[...], (8, LANES))
    got = gather_columns(tbl, slice(0, 8), index, 2)
    amount = jnp.where(way == 0, count[0], jnp.where(way == 1, count[1], jnp.where(way == 2, count[2], count[3])))
    step = jnp.where((way & 1) == 0, -1.0, 1.0).astype(f32)
    got = got + jnp.where(row == (way >> 1), step, 0.0)
    got = jnp.where((row == 3) & ((lane & 31) >= amount), -1.0, got)
    out[:, lanes(0)] = got
    out[:, lanes(1)] = gather_columns(tbl, slice(0, 8), jnp.broadcast_to(border[...], (8, LANES)), 2)


PLACE = {1: 3, 7: 4, 0: 5, 3: 6, 6: 7, 2: 8, 5: 9, 8: 10}


def edges_kernel(pos, spec, key, xp, xn, yp, yn, nbr, border, geo, bgeo, vcol, kinds, occ, tbl):
    tbl[...] = jnp.zeros_like(tbl)
    tbl[0:3, 0:256] = pos[...]
    tbl[3:4, 0:256] = spec[...].astype(f32)
    tbl[4:5, 0:256] = (key[...] == 0).astype(f32)
    row = lax.broadcasted_iota(jnp.int32, (8, LANES), 0)
    way = lax.broadcasted_iota(jnp.int32, (8, LANES), 1) >> 5
    came = jnp.where(
        way == 0,
        xp[:, lanes(0)],
        jnp.where(way == 1, xn[:, lanes(0)], jnp.where(way == 2, yp[:, lanes(0)], yn[:, lanes(0)])),
    )
    tbl[:, lanes(2)] = came
    tbl[4:5, lanes(2)] = (came[3:4] >= 0).astype(f32)

    def ghost(place, block, dx, dy):
        moved = block + jnp.where(row == 0, dx, jnp.where(row == 1, dy, jnp.where(row == 4, 1.0, 0.0)))
        tbl[:, lanes(place)] = moved

    ghost(3, xp[:, lanes(1)], -1.0, 0.0)
    ghost(4, xn[:, lanes(1)], 1.0, 0.0)
    for base, got, dy in ((5, yp, -1.0), (8, yn, 1.0)):
        ghost(base, got[:, lanes(2)], -1.0, dy)
        ghost(base + 1, got[:, lanes(1)], 0.0, dy)
        ghost(base + 2, got[:, lanes(3)], 1.0, dy)
    kinds[...] = jnp.maximum(tbl[3:4, :], 0.0)
    occ[...] = tbl[4:5, 0 : LOCAL * LANES]
    geo[...] = jnp.zeros_like(geo)
    vcol[...] = jnp.full_like(vcol, -1)
    for b in range(LOCAL):
        own = tbl[:, lanes(b)]
        for s in range(SLOTS):
            n = nbr[s : s + 1, lanes(b)]
            old = n >> 7
            block = jnp.minimum(old, 2)
            for was, now in PLACE.items():
                block = jnp.where(old == was + 3, now, block)
            col = jnp.maximum(block, 0) * 128 + (n & 127)
            got = gather_columns(tbl, slice(0, 8), jnp.broadcast_to(col, (8, LANES)), 11)
            valid = (n >= 0) & (got[4:5] > 0.5) & (own[4:5] > 0.5)
            off = got - own
            val = jnp.where(row < 3, off, jnp.where(jnp.broadcast_to(valid, (8, LANES)), got, -1.0))
            geo[b, pl.ds(s, 4, stride=16), :] = val[0:4]
            vcol[b, s : s + 1, :] = jnp.where(valid, col, -1)
    index = jnp.broadcast_to(border[...], (8, LANES))
    low = index & 127
    for t in range(8):
        rows = slice(t * 8, t * 8 + 8)
        bgeo[rows, :] = jnp.where(
            (index >> 7) == 0, take_lanes(geo[0, rows, :], low), take_lanes(geo[1, rows, :], low)
        )


def geometry(ox, oy, oz):
    d = jnp.sqrt(ox * ox + oy * oy + oz * oz + 1.0)
    rd = 1.0 / d
    u = (ox * rd, oy * rd, oz * rd)
    t = d * (1.0 / RADIUS)
    t2 = t * t
    t5 = t2 * t2 * t
    t6 = t5 * t
    env = 1.0 - 28.0 * t6 + 48.0 * t6 * t - 21.0 * t6 * t2
    theta = (math.pi / RADIUS) * d
    s1, c1 = jnp.sin(theta), jnp.cos(theta)
    sines, cosines = [s1], [c1]
    before_s, before_c = jnp.zeros_like(s1), jnp.ones_like(c1)
    for _ in range(7):
        ns = 2.0 * c1 * sines[-1] - before_s
        nc = 2.0 * c1 * cosines[-1] - before_c
        before_s, before_c = sines[-1], cosines[-1]
        sines.append(ns)
        cosines.append(nc)
    slope = (-168.0 * t5 + 336.0 * t6 - 168.0 * t6 * t) * (1.0 / RADIUS)
    return u, d, rd, env, slope, sines, cosines


def harmonics(u):
    x, y, z = u
    return [
        R3 * x,
        R3 * y,
        R3 * z,
        R15 * x * y,
        R15 * y * z,
        0.5 * R5 * (2.0 * z * z - x * x - y * y),
        R15 * x * z,
        0.5 * R15 * (x * x - y * y),
    ]


def place_geometry(geo, yref, basrow, bas):
    u, d, rd, env, slope, sines, cosines = geo
    for k, h in enumerate(harmonics(u)):
        yref[k * 16 : k * 16 + 16, :] = h
    factor = SCALE * env * rd
    for m in range(8):
        basrow[m * 16 : m * 16 + 16, :] = sines[m] * factor
    for s in range(SLOTS):
        got = basrow[pl.ds(s, 8, stride=16), :]
        bas[0:8, lanes(s)] = got
        bas[8:16, lanes(s)] = got - got.astype(bf16).astype(f32)


def geometry_back(geo, dyref, dbas):
    (x, y, z), d, rd, env, slope, sines, cosines = geo
    g = [dyref[k * 16 : k * 16 + 16, :] for k in range(8)]
    dx = R3 * g[0] + R15 * (y * g[3] + z * g[6] + x * g[7]) - R5 * x * g[5]
    dy = R3 * g[1] + R15 * (x * g[3] + z * g[4] - y * g[7]) - R5 * y * g[5]
    dz = R3 * g[2] + R15 * (y * g[4] + x * g[6]) + 2.0 * R5 * z * g[5]
    along = jnp.zeros_like(x)
    turned = jnp.zeros_like(x)
    for m in range(8):
        db = dbas[m * 16 : m * 16 + 16, :]
        along = along + db * sines[m]
        turned = turned + ((m + 1) * math.pi / RADIUS) * db * cosines[m]
    dd = SCALE * rd * (turned * env + along * (slope - env * rd))
    dd = dd - (dx * x + dy * y + dz * z) * rd
    return dx * rd + x * dd, dy * rd + y * dd, dz * rd + z * dd


def radial_forward(bas, first, second, third, wref, e1=None, e2=None):
    pre = mm(first[...], bas[...].astype(bf16))
    h, e = silu_parts(pre[:HID] + pre[HID:])
    if e1 is not None:
        e1[...] = e
    h, e = silu_parts(mm(second[...], split3(h)))
    if e2 is not None:
        e2[...] = e
    h = split3(h)
    for p in range(third.shape[0] // CH):
        wref[p * CH : (p + 1) * CH, :] = mm(third[p * CH : (p + 1) * CH, :], h)


def radial_back(dwref, third_t, second_t, first_t, e1, e2, dbrow, dbas):
    both = mm(third_t[...], dwref[...])
    dp = (both[:HID] + both[HID:]) * e2[...]
    dp = mm(second_t[...], split3(dp)) * e1[...]
    dbrow[...] = mm(first_t[...], split3(dp))
    dbas[...] = jnp.zeros_like(dbas)
    for s in range(SLOTS):
        dbas[pl.ds(s, 8, stride=16), :] = dbrow[0:8, lanes(s)]


ORDERS = ((0, 1), (1, 3), (4, 5))


def mixed(matrices, values, out):
    for l, (start, n) in enumerate(ORDERS):
        out[:, lanes(start, n)] = mm(matrices[l], split3(values[:, lanes(start, n)]))


def sum_of(terms):
    total = terms[0]
    for t in terms[1:]:
        total = total + t
    return total


def first_features(geo, emb, fref):
    iota = lax.broadcasted_iota(jnp.int32, (CH, LANES), 0)
    for s in range(SLOTS):
        kind = geo[0, 48 + s : 49 + s, :].astype(jnp.int32)
        hot = (iota == kind).astype(f32).astype(bf16)
        both = mm(emb[...], hot)
        fref[:, lanes(s)] = both[:CH] + both[CH:]


def layer_one_kernel(geo, kinds, first, second, third, emb, mf, mo, coef, out, keep, yref, basrow, bas, wref, fref, aref):
    place_geometry(geometry(geo[0, 0:16, :], geo[0, 16:32, :], geo[0, 32:48, :]), yref, basrow, bas)
    radial_forward(bas, first, second, third, wref)
    first_features(geo, emb, fref)

    def messages(c, _):
        acc = [None] * 9

        def add(k, v):
            acc[k] = v if acc[k] is None else acc[k] + v

        r0 = pl.ds(pl.multiple_of(c * 16, 16), 16)
        r1 = pl.ds(pl.multiple_of(c * 16 + CH, 16), 16)
        r2 = pl.ds(pl.multiple_of(c * 16 + 2 * CH, 16), 16)
        for s in range(SLOTS):
            f = fref[r0, lanes(s)]
            add(0, wref[r0, lanes(s)] * f)
            w1 = wref[r1, lanes(s)] * f
            w2 = wref[r2, lanes(s)] * f
            for k in range(8):
                add(k + 1, (w1 if k < 3 else w2) * yref[k * 16 + s : k * 16 + s + 1, :])
        for k in range(9):
            aref[r0, lanes(k)] = acc[k] * (1.0 / SLOTS)
        return 0

    lax.fori_loop(0, CH // 16, messages, 0)
    mixed(mf, aref, keep.at[0])
    p = [keep[0, :, lanes(k)] for k in range(9)]
    c = [coef[:, k : k + 1] for k in range(5)]
    aref[:, lanes(0)] = (
        p[0]
        + c[0] * p[0] * p[0]
        + c[1] * sum_of([p[k] * p[k] for k in range(1, 4)])
        + c[2] * sum_of([p[k] * p[k] for k in range(4, 9)])
    )
    up, ut = 1.0 + c[3] * p[0], 1.0 + c[4] * p[0]
    for k in range(1, 9):
        aref[:, lanes(k)] = p[k] * (up if k < 4 else ut)
    iota = lax.broadcasted_iota(jnp.int32, (CH, LANES), 0)
    hot = (iota == kinds[...].astype(jnp.int32)).astype(f32).astype(bf16)
    both = mm(emb[...], hot)
    out[0:CH, :] = (mm(mo[0], split3(aref[:, lanes(0)])) + (both[:CH] + both[CH:])).astype(bf16)
    for l, (start, n) in enumerate(ORDERS[1:], 1):
        got = mm(mo[l], split3(aref[:, lanes(start, n)]))
        for k in range(n):
            out[(start + k) * CH : (start + k + 1) * CH, :] = got[:, lanes(k)].astype(bf16)


def whole(a):
    rank = len(a.shape)
    return pl.BlockSpec(a.shape, lambda i: (0,) * rank)


def layer_one(geo, kinds, start, weights):
    n = geo.shape[0]
    first, second, third = weights["r1"]
    consts = (first, second, third, weights["emb"], weights["mf1"], weights["of1"], weights["coef1"])
    return call(
        layer_one_kernel,
        (shape(9 * CH, n * LANES, kind=bf16), shape(n, CH, 9 * LANES)),
        grid=(n,),
        in_specs=[
            pl.BlockSpec((1, 64, LANES), lambda i: (i, 0, 0)),
            pl.BlockSpec((1, LANES), lambda i: (0, i + start)),
        ]
        + [whole(a) for a in consts],
        out_specs=(
            pl.BlockSpec((9 * CH, LANES), lambda i: (0, i)),
            pl.BlockSpec((1, CH, 9 * LANES), lambda i: (i, 0, 0)),
        ),
        scratch=[
            pltpu.VMEM((128, LANES), f32),
            pltpu.VMEM((128, LANES), f32),
            pltpu.VMEM((16, EDGES), f32),
            pltpu.VMEM((3 * CH, EDGES), f32),
            pltpu.VMEM((CH, EDGES), f32),
            pltpu.VMEM((CH, 9 * LANES), f32),
        ],
        flops=n * 900000000,
    )(geo, kinds, *consts)


def layer_one_back_kernel(
    geo, grad, keep, first, second, third, third_t, second_t, first_t, emb, mb, mo, coef,
    out, yref, basrow, bas, wref, fref, aref, dref, e1, e2, dwref, dyref, dbrow, dbas,
):
    geom = geometry(geo[0, 0:16, :], geo[0, 16:32, :], geo[0, 32:48, :])
    place_geometry(geom, yref, basrow, bas)
    radial_forward(bas, first, second, third, wref, e1, e2)
    first_features(geo, emb, fref)
    for k in range(9):
        aref[:, lanes(k)] = grad[k * CH : (k + 1) * CH, :]
    mixed(mo, aref, dref)
    p = [keep[0, :, lanes(k)] for k in range(9)]
    g = [dref[:, lanes(k)] for k in range(9)]
    c = [coef[:, k : k + 1] for k in range(5)]
    aref[:, lanes(0)] = (
        g[0] * (1.0 + 2.0 * c[0] * p[0])
        + c[3] * sum_of([p[k] * g[k] for k in range(1, 4)])
        + c[4] * sum_of([p[k] * g[k] for k in range(4, 9)])
    )
    up, ut = 1.0 + c[3] * p[0], 1.0 + c[4] * p[0]
    vp, vt = 2.0 * c[1] * g[0], 2.0 * c[2] * g[0]
    for k in range(1, 9):
        aref[:, lanes(k)] = g[k] * (up if k < 4 else ut) + p[k] * (vp if k < 4 else vt)
    mixed(mb, aref, dref)
    dref[...] = dref[...] * (1.0 / SLOTS)
    dyref[...] = jnp.zeros_like(dyref)

    def slot(s, _):
        here = pl.ds(pl.multiple_of(s * LANES, LANES), LANES)
        y = [yref[pl.ds(k * 16 + s, 1), :] for k in range(8)]
        dy = [None] * 8
        for c in range(CH // 16):
            r0, r1, r2 = (slice(q * CH + c * 16, q * CH + c * 16 + 16) for q in range(3))
            f = fref[r0, here]
            w1 = wref[r1, here] * f
            w2 = wref[r2, here] * f
            d = [dref[r0, lanes(k)] for k in range(9)]
            dwref[r0, here] = (d[0] * f).astype(bf16)
            dwref[r1, here] = (f * sum_of([d[k + 1] * y[k] for k in range(3)])).astype(bf16)
            dwref[r2, here] = (f * sum_of([d[k + 1] * y[k] for k in range(3, 8)])).astype(bf16)
            for k in range(8):
                v = (w1 if k < 3 else w2) * d[k + 1]
                v = v[0:8] + v[8:16]
                dy[k] = v if dy[k] is None else dy[k] + v
        for k in range(8):
            dyref[pl.ds(k * 16 + s, 1), :] = jnp.sum(dy[k], axis=0, keepdims=True)
        return 0

    lax.fori_loop(0, SLOTS, slot, 0)
    radial_back(dwref, third_t, second_t, first_t, e1, e2, dbrow, dbas)
    dx, dy, dz = geometry_back(geom, dyref, dbas)
    out[0, 0:16, :] = dx
    out[0, 16:32, :] = dy
    out[0, 32:48, :] = dz


def layer_one_back(geo, grad, start, keep, weights):
    n = geo.shape[0]
    first, second, third = weights["r1"]
    consts = (first, second, third) + weights["b1"] + (
        weights["emb"], weights["mb1"], weights["ob1"], weights["coef1"])
    return call(
        layer_one_back_kernel,
        shape(n, 48, LANES),
        grid=(n,),
        in_specs=[
            pl.BlockSpec((1, 64, LANES), lambda i: (i, 0, 0)),
            pl.BlockSpec((9 * CH, LANES), lambda i: (0, i + start)),
            pl.BlockSpec((1, CH, 9 * LANES), lambda i: (i, 0, 0)),
        ]
        + [whole(a) for a in consts],
        out_specs=pl.BlockSpec((1, 48, LANES), lambda i: (i, 0, 0)),
        scratch=[
            pltpu.VMEM((128, LANES), f32),
            pltpu.VMEM((128, LANES), f32),
            pltpu.VMEM((16, EDGES), f32),
            pltpu.VMEM((3 * CH, EDGES), f32),
            pltpu.VMEM((CH, EDGES), f32),
            pltpu.VMEM((CH, 9 * LANES), f32),
            pltpu.VMEM((CH, 9 * LANES), f32),
            pltpu.VMEM((HID, EDGES), f32),
            pltpu.VMEM((HID, EDGES), f32),
            pltpu.VMEM((3 * CH, EDGES), bf16),
            pltpu.VMEM((128, LANES), f32),
            pltpu.VMEM((16, EDGES), f32),
            pltpu.VMEM((128, LANES), f32),
        ],
        flops=n * 2000000000,
    )(geo, grad, keep, *consts)


def build_hot(vcol, b, hot):
    iota = lax.broadcasted_iota(jnp.int32, (COLS, LANES), 0)

    def one(s, _):
        v = vcol[b, pl.ds(s, 1), :]
        hot[:, pl.ds(pl.multiple_of(s * LANES, LANES), LANES)] = (iota == v).astype(f32).astype(bf16)
        return 0

    lax.fori_loop(0, SLOTS, one, 0)


def layer_two_kernel(
    tl, tx, ty, geo, vcol, occ, first, second, third, third_t, second_t, first_t, mf, mb, of, ob,
    coef, lin, rh, rht, ro, energy, dtab, dgeo,
    tab, yref, basrow, bas, wref, aref, dref, e1, e2, dwref, dyref, dbrow, dbas, hot, gat, dgat,
):
    tab[:, 0:384] = tl[...]
    tab[:, 384:640] = tx[...]
    tab[:, 640:1408] = ty[...]
    dtab[...] = jnp.zeros_like(dtab)
    dyref[...] = jnp.zeros_like(dyref)

    def block(b, _):
        rows16 = lambda k: geo[b, k * 16 : k * 16 + 16, :]
        geom = geometry(rows16(0), rows16(1), rows16(2))
        place_geometry(geom, yref, basrow, bas)
        radial_forward(bas, first, second, third, wref, e1, e2)
        build_hot(vcol, b, hot)

        def gather(j, _):
            here = pl.ds(pl.multiple_of(j * 256, 256), 256)
            gat[:, here] = mm(tab[...], hot[:, here]).astype(bf16)
            return 0

        lax.fori_loop(0, EDGES // 256, gather, 0)

        def messages(c, _):
            acc = [None] * 9

            def add(k, v):
                acc[k] = v if acc[k] is None else acc[k] + v

            r = [pl.ds(pl.multiple_of(c * 16 + q * CH, 16), 16) for q in range(9)]
            for s in range(SLOTS):
                y = [yref[k * 16 + s : k * 16 + s + 1, :] for k in range(8)]
                x = [gat[r[q], lanes(s)].astype(f32) for q in range(9)]
                w = [wref[r[q], lanes(s)] for q in range(7)]
                a1 = sum_of([y[k] * x[k + 1] for k in range(3)])
                a2 = sum_of([y[k] * x[k + 1] for k in range(3, 8)])
                add(0, w[0] * x[0] + w[1] * a1 + w[2] * a2)
                t1, t2 = w[3] * x[0], w[5] * x[0]
                for k in range(8):
                    add(k + 1, (t1 if k < 3 else t2) * y[k] + (w[4] if k < 3 else w[6]) * x[k + 1])
            for k in range(9):
                aref[r[0], lanes(k)] = acc[k] * (1.0 / SLOTS)
            return 0

        lax.fori_loop(0, CH // 16, messages, 0)
        mixed(mf, aref, dref)
        p = [dref[:, lanes(k)] for k in range(9)]
        c = [coef[:, k : k + 1] for k in range(3)]
        prod = (
            p[0]
            + c[0] * p[0] * p[0]
            + c[1] * sum_of([p[k] * p[k] for k in range(1, 4)])
            + c[2] * sum_of([p[k] * p[k] for k in range(4, 9)])
        )
        ownl = pl.ds(pl.multiple_of(b * LANES, LANES), LANES)
        base = tab[0:CH, ownl].astype(f32)
        scal = mm(of[...], split3(prod)) + base
        h, e = silu_parts(mm(rht[...], split3(scal)))
        mask = occ[:, ownl]
        tot = jnp.sum(ro[...] * h, axis=0, keepdims=True) + jnp.sum(lin[...] * base, axis=0, keepdims=True)
        energy[:, ownl] = tot * mask
        ds = mm(rh[...], split3(ro[...] * e * mask))
        dtab[0:CH, ownl] = dtab[0:CH, ownl] + ds + lin[...] * mask
        db = mm(ob[...], split3(ds))
        aref[:, lanes(0)] = db * (1.0 + 2.0 * c[0] * p[0])
        for k in range(1, 9):
            aref[:, lanes(k)] = 2.0 * (c[1] if k < 4 else c[2]) * p[k] * db
        mixed(mb, aref, dref)
        dref[...] = dref[...] * (1.0 / SLOTS)

        def slot(s, _):
            here = pl.ds(pl.multiple_of(s * LANES, LANES), LANES)
            y = [yref[pl.ds(k * 16 + s, 1), :] for k in range(8)]
            dy = [None] * 8
            for cc in range(CH // 16):
                r = [slice(q * CH + cc * 16, q * CH + cc * 16 + 16) for q in range(9)]
                x = [gat[r[q], here].astype(f32) for q in range(9)]
                w = [wref[r[q], here] for q in range(7)]
                d = [dref[r[0], lanes(k)] for k in range(9)]
                t1 = sum_of([y[k] * d[k + 1] for k in range(3)])
                t2 = sum_of([y[k] * d[k + 1] for k in range(3, 8)])
                a1 = sum_of([y[k] * x[k + 1] for k in range(3)])
                a2 = sum_of([y[k] * x[k + 1] for k in range(3, 8)])
                b1 = sum_of([d[k + 1] * x[k + 1] for k in range(3)])
                b2 = sum_of([d[k + 1] * x[k + 1] for k in range(3, 8)])
                dgat[r[0], here] = (w[0] * d[0] + w[3] * t1 + w[5] * t2).astype(bf16)
                m1, m2 = w[1] * d[0], w[2] * d[0]
                n1, n2 = w[3] * x[0], w[5] * x[0]
                for k in range(8):
                    m, n, q = (m1, n1, w[4]) if k < 3 else (m2, n2, w[6])
                    dgat[r[k + 1], here] = (m * y[k] + q * d[k + 1]).astype(bf16)
                    v = m * x[k + 1] + n * d[k + 1]
                    v = v[0:8] + v[8:16]
                    dy[k] = v if dy[k] is None else dy[k] + v
                for q, v in enumerate((d[0] * x[0], d[0] * a1, d[0] * a2, x[0] * t1, b1, x[0] * t2, b2)):
                    dwref[r[q], here] = v.astype(bf16)
            for k in range(8):
                dyref[pl.ds(k * 16 + s, 1), :] = jnp.sum(dy[k], axis=0, keepdims=True)
            return 0

        lax.fori_loop(0, SLOTS, slot, 0)

        def scatter(j, _):
            here = pl.ds(pl.multiple_of(j * 256, 256), 256)
            dtab[:, here] = dtab[:, here] + mm_nt(dgat[...], hot[here, :])
            return 0

        lax.fori_loop(0, COLS // 256, scatter, 0)
        rest = COLS // 256 * 256
        dtab[:, rest:COLS] = dtab[:, rest:COLS] + mm_nt(dgat[...], hot[rest:COLS, :])
        radial_back(dwref, third_t, second_t, first_t, e1, e2, dbrow, dbas)
        dx, dy, dz = geometry_back(geom, dyref, dbas)
        dgeo[b, 0:16, :] = dx
        dgeo[b, 16:32, :] = dy
        dgeo[b, 32:48, :] = dz
        return 0

    lax.fori_loop(0, LOCAL, block, 0)


def layer_two(tl, tx, ty, geo, vcol, occ, w):
    first, second, third = w["r2"]
    return call(
        layer_two_kernel,
        (shape(1, LOCAL * LANES), shape(9 * CH, COLS), shape(LOCAL, 48, LANES)),
        scratch=[
            pltpu.VMEM((9 * CH, COLS), bf16),
            pltpu.VMEM((128, LANES), f32),
            pltpu.VMEM((128, LANES), f32),
            pltpu.VMEM((16, EDGES), f32),
            pltpu.VMEM((7 * CH, EDGES), f32),
            pltpu.VMEM((CH, 9 * LANES), f32),
            pltpu.VMEM((CH, 9 * LANES), f32),
            pltpu.VMEM((HID, EDGES), f32),
            pltpu.VMEM((HID, EDGES), f32),
            pltpu.VMEM((7 * CH, EDGES), bf16),
            pltpu.VMEM((128, LANES), f32),
            pltpu.VMEM((16, EDGES), f32),
            pltpu.VMEM((128, LANES), f32),
            pltpu.VMEM((COLS, EDGES), bf16),
            pltpu.VMEM((9 * CH, EDGES), bf16),
            pltpu.VMEM((9 * CH, EDGES), bf16),
        ],
        flops=40000000000,
    )(tl, tx, ty, geo, vcol, occ, first, second, third, *w["b2"], w["mf2"], w["mb2"], w["of2"],
      w["ob2"], w["coef2"], w["lin"], w["rh"], w["rht"], w["ro"])


def split_rows(x):
    hi = x.astype(bf16).astype(f32)
    rest = x - hi
    mid = rest.astype(bf16).astype(f32)
    return hi, mid, rest - mid


def place_border(x, border):
    slots = lax.broadcasted_iota(jnp.int32, (2 * LANES, LANES), 0)
    hot = (slots == border[...]).astype(f32).astype(bf16)
    n = x.shape[0]
    got = mm_nt(jnp.concatenate(split_rows(x), axis=0).astype(bf16), hot)
    return got[:n] + got[n : 2 * n] + got[2 * n :]


def columns_kernel(g2, g1, b0, b1, b2, b3, vcol, border, out, tot, lhs, hot):
    tot[...] = jnp.zeros_like(tot)
    for b in range(LOCAL):
        tot[b, 0:48, :] = g2[b] + g1[b]
    placed = place_border(b0[...] + b1[...] + (b2[...] + b3[...]), border)
    for b in range(2):
        tot[b, 0:48, :] = tot[b, 0:48, :] + placed[:, lanes(b)]
    out[...] = jnp.zeros_like(out)

    def block(b, _):
        build_hot(vcol, b, hot)
        lhs[...] = jnp.zeros_like(lhs)
        own = jnp.zeros((4, LANES), f32)
        for s in range(SLOTS):
            x = tot[b, pl.ds(s, 4, stride=16), :]
            own = own + x
            for q, part in enumerate(split_rows(x)):
                lhs[q * 8 : q * 8 + 4, lanes(s)] = part
        got = mm_nt(lhs[...].astype(bf16), hot[...])
        out[...] = out[...] + (got[0:8] + got[8:16] + got[16:24])
        ownl = pl.ds(pl.multiple_of(b * LANES, LANES), LANES)
        out[0:4, ownl] = out[0:4, ownl] - own
        return 0

    lax.fori_loop(0, LOCAL, block, 0)


def forces_kernel(col, r1, r2, xp, xn, border, out):
    total = xp[...] + xn[...] + (r1[:, lanes(1)] + r2[:, lanes(1)])
    placed = place_border(total, border)
    out[:, 0:256] = -(col[0:3, 0:256] + placed[0:3])
    out[:, 256:384] = -col[0:3, 256:384]


def from_behind(block, axis, distance):
    count = lax.axis_size(axis)
    route = [((i - distance) % count, i) for i in range(count)]
    return lax.ppermute(block, axis, route)


def rounded(x):
    hi = lax.reduce_precision(x, 8, 7)
    return hi.astype(bf16), (x - hi).astype(bf16)


def left3(x):
    hi, lo = rounded(x)
    return jnp.concatenate([hi, hi, lo], axis=-1)


def prepare(embedding, radial_in, radial_mid, outs, mix, mix_out_one, mix_out_two, product_one, product_two, read_lin, read_hidden, read_out):
    w = {}
    for t in range(2):
        hi, lo = rounded(radial_in[t].T)
        first = jnp.concatenate(
            [jnp.concatenate([hi, hi], axis=1), jnp.concatenate([lo, jnp.zeros_like(lo)], axis=1)], axis=0)
        name = str(t + 1)
        w["r" + name] = (first, left3(radial_mid[t].T), left3(outs[t].T))
        back_in = jnp.concatenate([radial_in[t], jnp.zeros_like(radial_in[t])], axis=0)
        w["b" + name] = (jnp.concatenate(rounded(outs[t]), axis=0), left3(radial_mid[t]), left3(back_in))
        w["mf" + name] = left3(jnp.swapaxes(mix[t], 1, 2))
        w["mb" + name] = left3(mix[t])
    w["of1"] = left3(jnp.swapaxes(mix_out_one, 1, 2))
    w["ob1"] = left3(mix_out_one)
    w["of2"] = left3(mix_out_two.T)
    w["ob2"] = left3(mix_out_two)
    w["coef1"] = product_one.T
    w["coef2"] = product_two.T
    padded = jnp.pad(embedding, ((0, CH - embedding.shape[0]), (0, 0))).T
    w["emb"] = jnp.concatenate(rounded(padded), axis=0)
    w["lin"] = read_lin[:, None]
    w["rh"] = left3(read_hidden)
    w["rht"] = left3(read_hidden.T)
    w["ro"] = read_out[:, None]
    return w


def on_device(
    positions, species, dest_key, send_list, send_count, border, neighbours, embedding, radial_in,
    radial_mid, radial_out_one, radial_out_two, mix, mix_out_one, mix_out_two, product_one,
    product_two, read_lin, read_hidden, read_out,
):
    pos = positions[0, 0]
    spec = species[0]
    key = dest_key[0]
    rows = border[0]
    nbr = neighbours[0, 0].T
    packet = call(
        packet_kernel,
        shape(8, 256),
        scratch=[pltpu.VMEM((8, 256), f32)],
        in_specs=[VMEM, VMEM, VMEM, VMEM, SMEM],
    )(pos, spec, send_list.reshape(1, LANES), rows, send_count.reshape(4))
    xp = from_behind(packet, "gx", 1)
    xn = from_behind(packet, "gx", -1)
    wide = jnp.concatenate([packet, xp[:, LANES:], xn[:, LANES:]], axis=1)
    yp = from_behind(wide, "gy", 1)
    yn = from_behind(wide, "gy", -1)
    w = prepare(embedding, radial_in, radial_mid, (radial_out_one, radial_out_two), mix, mix_out_one,
                mix_out_two, product_one, product_two, read_lin, read_hidden, read_out)
    geo, bgeo, vcol, kinds, occ = call(
        edges_kernel,
        (
            shape(LOCAL, 64, LANES),
            shape(64, LANES),
            shape(LOCAL, 16, LANES, kind=jnp.int32),
            shape(1, COLS),
            shape(1, LOCAL * LANES),
        ),
        scratch=[pltpu.VMEM((8, COLS), f32)],
    )(pos, spec, key, xp, xn, yp, yn, nbr, rows)
    gxp = from_behind(bgeo, "gx", 1)
    gxn = from_behind(bgeo, "gx", -1)
    tl, kl = layer_one(geo, kinds, 0, w)
    three = jnp.stack([gxp, bgeo, gxn])
    gyp = from_behind(three, "gy", 1)
    gyn = from_behind(three, "gy", -1)
    geo_x = jnp.stack([gxp, gxn])
    tx, kx = layer_one(geo_x, kinds, 3, w)
    geo_y = jnp.concatenate([gyp, gyn], axis=0)
    ty, ky = layer_one(geo_y, kinds, 5, w)
    energy, dtab, g2 = layer_two(tl, tx, ty, geo, vcol, occ, w)
    dgy = layer_one_back(geo_y, dtab, 5, ky, w)
    ry1 = from_behind(dgy[0:3], "gy", -1)
    ry2 = from_behind(dgy[3:6], "gy", 1)
    dgx = layer_one_back(geo_x, dtab, 3, kx, w)
    rx1 = from_behind(dgx[0] + ry1[0] + ry2[0], "gx", -1)
    rx2 = from_behind(dgx[1] + ry1[2] + ry2[2], "gx", 1)
    g1 = layer_one_back(geo, dtab, 0, kl, w)
    col = call(
        columns_kernel,
        shape(8, COLS),
        scratch=[
            pltpu.VMEM((LOCAL, 64, LANES), f32),
            pltpu.VMEM((24, EDGES), f32),
            pltpu.VMEM((COLS, EDGES), bf16),
        ],
    )(g2, g1, ry1[1], ry2[1], rx1, rx2, vcol, rows)
    r1 = from_behind(col[:, 640:1024], "gy", -1)
    r2 = from_behind(col[:, 1024:1408], "gy", 1)
    sx1 = from_behind(col[:, 384:512] + r1[:, 0:128] + r2[:, 0:128], "gx", -1)
    sx2 = from_behind(col[:, 512:640] + r1[:, 256:384] + r2[:, 256:384], "gx", 1)
    forces = call(forces_kernel, shape(3, LOCAL * LANES))(col, r1, r2, sx1, sx2, rows)
    return energy[None], forces[None, None]


def solution(mesh):
    along = P("gx", "gy")
    in_specs = (along,) * 7 + (P(),) * 13
    return jax.shard_map(
        on_device, mesh=mesh, in_specs=in_specs, out_specs=(along, along), check_vma=False
    )
```

```python
import functools
import math

import jax
import jax.numpy as jnp
from jax import lax
from jax.experimental import pallas as pl
from jax.experimental.pallas import tpu as pltpu
from jax.sharding import PartitionSpec as P

f32 = jnp.float32
bf16 = jnp.bfloat16
CH = 128
HID = 64
SLOTS = 12
LANES = 128
EDGES = SLOTS * LANES
LOCAL = 3
COLS = 11 * LANES
NL, NX, NY = 3, 2, 2
RADIUS = 5.0
SCALE = math.sqrt(2.0 / RADIUS)
R3 = math.sqrt(3.0)
R5 = math.sqrt(5.0)
R15 = math.sqrt(15.0)
VMEM = pl.BlockSpec(memory_space=pltpu.VMEM)
SMEM = pl.BlockSpec(memory_space=pltpu.SMEM)
LIMIT = 60 * 1024 * 1024


def call(kernel, out_shape, scratch=(), flops=1000000, in_specs=None, **kw):
    return pl.pallas_call(
        kernel,
        out_shape=out_shape,
        scratch_shapes=list(scratch),
        compiler_params=pltpu.CompilerParams(vmem_limit_bytes=LIMIT),
        cost_estimate=pl.CostEstimate(flops=flops, bytes_accessed=1000000, transcendentals=0),
        **({"in_specs": in_specs} if in_specs is not None else {}),
        **kw,
    )


def shape(*dims, kind=f32):
    return jax.ShapeDtypeStruct(dims, kind)


def lanes(i, n=1):
    return slice(i * LANES, (i + n) * LANES)


def hi_lo(x):
    hi = x.astype(bf16)
    return hi, (x - hi.astype(f32)).astype(bf16)


def split3(x):
    hi, lo = hi_lo(x)
    return jnp.concatenate([hi, lo, hi], axis=0)


def mm(a, b):
    return jnp.dot(a, b, preferred_element_type=f32)


def mm_nt(a, b):
    return lax.dot_general(a, b, (((1,), (1,)), ((), ())), preferred_element_type=f32)


def silu_parts(x):
    s = 0.5 * jnp.tanh(0.5 * x) + 0.5
    h = x * s
    return h, s + h * (1.0 - s)


def take_lanes(chunk, index):
    return jnp.take_along_axis(chunk, index, axis=1, mode="promise_in_bounds")


def gather_columns(ref, rows, index, chunks):
    low = index & 127
    block = index >> 7
    out = take_lanes(ref[rows, lanes(0)], low)
    for c in range(1, chunks):
        out = jnp.where(block == c, take_lanes(ref[rows, lanes(c)], low), out)
    return out


def packet_kernel(pos, spec, listed, border, count, out, tbl):
    tbl[...] = jnp.zeros_like(tbl)
    tbl[0:3, :] = pos[...]
    tbl[3:4, :] = spec[...].astype(f32)
    row = lax.broadcasted_iota(jnp.int32, (8, LANES), 0)
    lane = lax.broadcasted_iota(jnp.int32, (8, LANES), 1)
    way = lane >> 5
    index = jnp.broadcast_to(listed[...], (8, LANES))
    got = gather_columns(tbl, slice(0, 8), index, 2)
    amount = jnp.where(way == 0, count[0], jnp.where(way == 1, count[1], jnp.where(way == 2, count[2], count[3])))
    step = jnp.where((way & 1) == 0, -1.0, 1.0).astype(f32)
    got = got + jnp.where(row == (way >> 1), step, 0.0)
    got = jnp.where((row == 3) & ((lane & 31) >= amount), -1.0, got)
    out[:, lanes(0)] = got
    out[:, lanes(1)] = gather_columns(tbl, slice(0, 8), jnp.broadcast_to(border[...], (8, LANES)), 2)


PLACE = {1: 3, 7: 4, 0: 5, 3: 6, 6: 7, 2: 8, 5: 9, 8: 10}


def edges_kernel(pos, spec, key, xp, xn, yp, yn, nbr, border, geo, bgeo, vcol, kinds, occ, tbl):
    tbl[...] = jnp.zeros_like(tbl)
    tbl[0:3, 0:256] = pos[...]
    tbl[3:4, 0:256] = spec[...].astype(f32)
    tbl[4:5, 0:256] = (key[...] == 0).astype(f32)
    row = lax.broadcasted_iota(jnp.int32, (8, LANES), 0)
    way = lax.broadcasted_iota(jnp.int32, (8, LANES), 1) >> 5
    came = jnp.where(
        way == 0,
        xp[:, lanes(0)],
        jnp.where(way == 1, xn[:, lanes(0)], jnp.where(way == 2, yp[:, lanes(0)], yn[:, lanes(0)])),
    )
    tbl[:, lanes(2)] = came
    tbl[4:5, lanes(2)] = (came[3:4] >= 0).astype(f32)

    def ghost(place, block, dx, dy):
        moved = block + jnp.where(row == 0, dx, jnp.where(row == 1, dy, jnp.where(row == 4, 1.0, 0.0)))
        tbl[:, lanes(place)] = moved

    ghost(3, xp[:, lanes(1)], -1.0, 0.0)
    ghost(4, xn[:, lanes(1)], 1.0, 0.0)
    for base, got, dy in ((5, yp, -1.0), (8, yn, 1.0)):
        ghost(base, got[:, lanes(2)], -1.0, dy)
        ghost(base + 1, got[:, lanes(1)], 0.0, dy)
        ghost(base + 2, got[:, lanes(3)], 1.0, dy)
    kinds[...] = jnp.maximum(tbl[3:4, :], 0.0)
    occ[...] = tbl[4:5, 0 : LOCAL * LANES]
    geo[...] = jnp.zeros_like(geo)
    vcol[...] = jnp.full_like(vcol, -1)
    for b in range(LOCAL):
        own = tbl[:, lanes(b)]
        for s in range(SLOTS):
            n = nbr[s : s + 1, lanes(b)]
            old = n >> 7
            block = jnp.minimum(old, 2)
            for was, now in PLACE.items():
                block = jnp.where(old == was + 3, now, block)
            col = jnp.maximum(block, 0) * 128 + (n & 127)
            got = gather_columns(tbl, slice(0, 8), jnp.broadcast_to(col, (8, LANES)), 11)
            valid = (n >= 0) & (got[4:5] > 0.5) & (own[4:5] > 0.5)
            off = got - own
            val = jnp.where(row < 3, off, jnp.where(jnp.broadcast_to(valid, (8, LANES)), got, -1.0))
            geo[b, pl.ds(s, 4, stride=16), :] = val[0:4]
            vcol[b, s : s + 1, :] = jnp.where(valid, col, -1)
    index = jnp.broadcast_to(border[...], (8, LANES))
    low = index & 127
    for t in range(8):
        rows = slice(t * 8, t * 8 + 8)
        bgeo[rows, :] = jnp.where(
            (index >> 7) == 0, take_lanes(geo[0, rows, :], low), take_lanes(geo[1, rows, :], low)
        )


def geometry(ox, oy, oz):
    d = jnp.sqrt(ox * ox + oy * oy + oz * oz + 1.0)
    rd = 1.0 / d
    u = (ox * rd, oy * rd, oz * rd)
    t = d * (1.0 / RADIUS)
    t2 = t * t
    t5 = t2 * t2 * t
    t6 = t5 * t
    env = 1.0 - 28.0 * t6 + 48.0 * t6 * t - 21.0 * t6 * t2
    theta = (math.pi / RADIUS) * d
    s1, c1 = jnp.sin(theta), jnp.cos(theta)
    sines, cosines = [s1], [c1]
    before_s, before_c = jnp.zeros_like(s1), jnp.ones_like(c1)
    for _ in range(7):
        ns = 2.0 * c1 * sines[-1] - before_s
        nc = 2.0 * c1 * cosines[-1] - before_c
        before_s, before_c = sines[-1], cosines[-1]
        sines.append(ns)
        cosines.append(nc)
    slope = (-168.0 * t5 + 336.0 * t6 - 168.0 * t6 * t) * (1.0 / RADIUS)
    return u, d, rd, env, slope, sines, cosines


def harmonics(u):
    x, y, z = u
    return [
        R3 * x,
        R3 * y,
        R3 * z,
        R15 * x * y,
        R15 * y * z,
        0.5 * R5 * (2.0 * z * z - x * x - y * y),
        R15 * x * z,
        0.5 * R15 * (x * x - y * y),
    ]


def place_geometry(geo, yref, basrow, bas):
    u, d, rd, env, slope, sines, cosines = geo
    for k, h in enumerate(harmonics(u)):
        yref[k * 16 : k * 16 + 16, :] = h
    factor = SCALE * env * rd
    for m in range(8):
        basrow[m * 16 : m * 16 + 16, :] = sines[m] * factor
    for s in range(SLOTS):
        got = basrow[pl.ds(s, 8, stride=16), :]
        bas[0:8, lanes(s)] = got
        bas[8:16, lanes(s)] = got - got.astype(bf16).astype(f32)


def geometry_back(geo, dyref, dbas):
    (x, y, z), d, rd, env, slope, sines, cosines = geo
    g = [dyref[k * 16 : k * 16 + 16, :] for k in range(8)]
    dx = R3 * g[0] + R15 * (y * g[3] + z * g[6] + x * g[7]) - R5 * x * g[5]
    dy = R3 * g[1] + R15 * (x * g[3] + z * g[4] - y * g[7]) - R5 * y * g[5]
    dz = R3 * g[2] + R15 * (y * g[4] + x * g[6]) + 2.0 * R5 * z * g[5]
    along = jnp.zeros_like(x)
    turned = jnp.zeros_like(x)
    for m in range(8):
        db = dbas[m * 16 : m * 16 + 16, :]
        along = along + db * sines[m]
        turned = turned + ((m + 1) * math.pi / RADIUS) * db * cosines[m]
    dd = SCALE * rd * (turned * env + along * (slope - env * rd))
    dd = dd - (dx * x + dy * y + dz * z) * rd
    return dx * rd + x * dd, dy * rd + y * dd, dz * rd + z * dd


def radial_forward(bas, first, second, third, wref, e1=None, e2=None):
    pre = mm(first[...], bas[...].astype(bf16))
    h, e = silu_parts(pre[:HID] + pre[HID:])
    if e1 is not None:
        e1[...] = e
    h, e = silu_parts(mm(second[...], split3(h)))
    if e2 is not None:
        e2[...] = e
    h = split3(h)
    for p in range(third.shape[0] // CH):
        wref[p * CH : (p + 1) * CH, :] = mm(third[p * CH : (p + 1) * CH, :], h)


def radial_back(dwref, third_t, second_t, first_t, e1, e2, dbrow, dbas):
    both = mm(third_t[...], dwref[...])
    dp = (both[:HID] + both[HID:]) * e2[...]
    dp = mm(second_t[...], split3(dp)) * e1[...]
    dbrow[...] = mm(first_t[...], split3(dp))
    dbas[...] = jnp.zeros_like(dbas)
    for s in range(SLOTS):
        dbas[pl.ds(s, 8, stride=16), :] = dbrow[0:8, lanes(s)]


ORDERS = ((0, 1), (1, 3), (4, 5))


def mixed(matrices, values, out):
    for l, (start, n) in enumerate(ORDERS):
        out[:, lanes(start, n)] = mm(matrices[l], split3(values[:, lanes(start, n)]))


def sum_of(terms):
    total = terms[0]
    for t in terms[1:]:
        total = total + t
    return total


def first_features(geo, emb, fref):
    iota = lax.broadcasted_iota(jnp.int32, (CH, LANES), 0)
    for s in range(SLOTS):
        kind = geo[48 + s : 49 + s, :].astype(jnp.int32)
        hot = (iota == kind).astype(f32).astype(bf16)
        both = mm(emb[...], hot)
        fref[:, lanes(s)] = both[:CH] + both[CH:]


def ctiles():
    return [slice(c * 16, c * 16 + 16) for c in range(CH // 16)]


def layer_one_kernel(many, geos, kinds, first, second, third, emb, mf, mo, coef, out, keeps, *scratch):
    sets = [scratch[6 * q : 6 * q + 6] for q in range(many)]
    for q, (yref, basrow, bas, wref, fref, aref) in enumerate(sets):
        geo = geos.at[q]
        place_geometry(geometry(geo[0:16, :], geo[16:32, :], geo[32:48, :]), yref, basrow, bas)
    for q, (yref, basrow, bas, wref, fref, aref) in enumerate(sets):
        radial_forward(bas, first, second, third, wref)
        first_features(geos.at[q], emb, fref)

    def messages(c, _):
        r0 = pl.ds(pl.multiple_of(c * 16, 16), 16)
        r1 = pl.ds(pl.multiple_of(c * 16 + CH, 16), 16)
        r2 = pl.ds(pl.multiple_of(c * 16 + 2 * CH, 16), 16)
        for yref, basrow, bas, wref, fref, aref in sets:
            acc = [None] * 9

            def add(k, v):
                acc[k] = v if acc[k] is None else acc[k] + v

            for s in range(SLOTS):
                f = fref[r0, lanes(s)]
                add(0, wref[r0, lanes(s)] * f)
                w1 = wref[r1, lanes(s)] * f
                w2 = wref[r2, lanes(s)] * f
                for k in range(8):
                    add(k + 1, (w1 if k < 3 else w2) * yref[k * 16 + s : k * 16 + s + 1, :])
            for k in range(9):
                aref[r0, lanes(k)] = acc[k] * (1.0 / SLOTS)
        return 0

    lax.fori_loop(0, CH // 16, messages, 0, unroll=True)
    for q in range(many):
        mixed(mf, sets[q][5], keeps.at[q])
    for q in range(many):
        keep, aref = keeps.at[q], sets[q][5]
        for r in ctiles():
            p = [keep[r, lanes(k)] for k in range(9)]
            c = [coef[r, k : k + 1] for k in range(5)]
            aref[r, lanes(0)] = (
                p[0]
                + c[0] * p[0] * p[0]
                + c[1] * sum_of([p[k] * p[k] for k in range(1, 4)])
                + c[2] * sum_of([p[k] * p[k] for k in range(4, 9)])
            )
            up, ut = 1.0 + c[3] * p[0], 1.0 + c[4] * p[0]
            for k in range(1, 9):
                aref[r, lanes(k)] = p[k] * (up if k < 4 else ut)
    iota = lax.broadcasted_iota(jnp.int32, (CH, LANES), 0)
    for q in range(many):
        aref = sets[q][5]
        hot = (iota == kinds[:, lanes(q)].astype(jnp.int32)).astype(f32).astype(bf16)
        both = mm(emb[...], hot)
        out[0:CH, lanes(q)] = (mm(mo[0], split3(aref[:, lanes(0)])) + (both[:CH] + both[CH:])).astype(bf16)
        for l, (start, n) in enumerate(ORDERS[1:], 1):
            got = mm(mo[l], split3(aref[:, lanes(start, n)]))
            for k in range(n):
                out[(start + k) * CH : (start + k + 1) * CH, lanes(q)] = got[:, lanes(k)].astype(bf16)


def whole(a):
    rank = len(a.shape)
    return pl.BlockSpec(a.shape, lambda i: (0,) * rank)


def layer_one(geo, kinds, many, weights):
    n = geo.shape[0]
    first, second, third = weights["r1"]
    consts = (first, second, third, weights["emb"], weights["mf1"], weights["of1"], weights["coef1"])
    return call(
        functools.partial(layer_one_kernel, many),
        (shape(9 * CH, n * LANES, kind=bf16), shape(n, CH, 9 * LANES)),
        grid=(n // many,),
        in_specs=[
            pl.BlockSpec((many, 64, LANES), lambda i: (i, 0, 0)),
            pl.BlockSpec((1, many * LANES), lambda i: (0, i)),
        ]
        + [whole(a) for a in consts],
        out_specs=(
            pl.BlockSpec((9 * CH, many * LANES), lambda i: (0, i)),
            pl.BlockSpec((many, CH, 9 * LANES), lambda i: (i, 0, 0)),
        ),
        scratch=[
            pltpu.VMEM((128, LANES), f32),
            pltpu.VMEM((128, LANES), f32),
            pltpu.VMEM((16, EDGES), f32),
            pltpu.VMEM((3 * CH, EDGES), f32),
            pltpu.VMEM((CH, EDGES), f32),
            pltpu.VMEM((CH, 9 * LANES), f32),
        ]
        * many,
        flops=n * 900000000,
    )(geo, kinds, *consts)


def layer_one_back_kernel(
    many, geos, grad, keeps, first, second, third, third_t, second_t, first_t, emb, mb, mo, coef, out, *scratch
):
    sets = [scratch[13 * q : 13 * q + 13] for q in range(many)]
    geoms = []
    for q in range(many):
        geo, (yref, basrow, bas) = geos.at[q], sets[q][:3]
        geoms.append(geometry(geo[0:16, :], geo[16:32, :], geo[32:48, :]))
        place_geometry(geoms[q], yref, basrow, bas)
    for q in range(many):
        yref, basrow, bas, wref, fref, aref, dref, e1, e2, dwref, dyref, dbrow, dbas = sets[q]
        radial_forward(bas, first, second, third, wref, e1, e2)
        first_features(geos.at[q], emb, fref)
    for q in range(many):
        aref, dref = sets[q][5:7]
        for k in range(9):
            aref[:, lanes(k)] = grad[k * CH : (k + 1) * CH, lanes(q)]
        mixed(mo, aref, dref)
    for q in range(many):
        aref, dref = sets[q][5:7]
        keep = keeps.at[q]
        for r in ctiles():
            p = [keep[r, lanes(k)] for k in range(9)]
            g = [dref[r, lanes(k)] for k in range(9)]
            c = [coef[r, k : k + 1] for k in range(5)]
            aref[r, lanes(0)] = (1.0 / SLOTS) * (
                g[0] * (1.0 + 2.0 * c[0] * p[0])
                + c[3] * sum_of([p[k] * g[k] for k in range(1, 4)])
                + c[4] * sum_of([p[k] * g[k] for k in range(4, 9)])
            )
            g = [v * (1.0 / SLOTS) for v in g]
            up, ut = 1.0 + c[3] * p[0], 1.0 + c[4] * p[0]
            vp, vt = 2.0 * c[1] * g[0], 2.0 * c[2] * g[0]
            for k in range(1, 9):
                aref[r, lanes(k)] = g[k] * (up if k < 4 else ut) + p[k] * (vp if k < 4 else vt)
    for q in range(many):
        mixed(mb, *sets[q][5:7])
        sets[q][10][...] = jnp.zeros_like(sets[q][10])

    def slot(s, _):
        here = pl.ds(pl.multiple_of(s * LANES, LANES), LANES)
        for yref, basrow, bas, wref, fref, aref, dref, e1, e2, dwref, dyref, dbrow, dbas in sets:
            y = [yref[pl.ds(k * 16 + s, 1), :] for k in range(8)]
            dy = [None] * 8
            for c in range(CH // 16):
                r0, r1, r2 = (slice(q * CH + c * 16, q * CH + c * 16 + 16) for q in range(3))
                f = fref[r0, here]
                w1 = wref[r1, here] * f
                w2 = wref[r2, here] * f
                d = [dref[r0, lanes(k)] for k in range(9)]
                dwref[r0, here] = (d[0] * f).astype(bf16)
                dwref[r1, here] = (f * sum_of([d[k + 1] * y[k] for k in range(3)])).astype(bf16)
                dwref[r2, here] = (f * sum_of([d[k + 1] * y[k] for k in range(3, 8)])).astype(bf16)
                for k in range(8):
                    v = (w1 if k < 3 else w2) * d[k + 1]
                    v = v[0:8] + v[8:16]
                    dy[k] = v if dy[k] is None else dy[k] + v
            for k in range(8):
                dyref[pl.ds(k * 16 + s, 1), :] = jnp.sum(dy[k], axis=0, keepdims=True)
        return 0

    lax.fori_loop(0, SLOTS, slot, 0, unroll=True)
    for yref, basrow, bas, wref, fref, aref, dref, e1, e2, dwref, dyref, dbrow, dbas in sets:
        radial_back(dwref, third_t, second_t, first_t, e1, e2, dbrow, dbas)
    for q in range(many):
        dx, dy, dz = geometry_back(geoms[q], sets[q][10], sets[q][12])
        out[q, 0:16, :] = dx
        out[q, 16:32, :] = dy
        out[q, 32:48, :] = dz


def layer_one_back(geo, grad, keep, many, weights):
    n = geo.shape[0]
    first, second, third = weights["r1"]
    consts = (first, second, third) + weights["b1"] + (
        weights["emb"], weights["mb1"], weights["ob1"], weights["coef1"])
    return call(
        functools.partial(layer_one_back_kernel, many),
        shape(n, 48, LANES),
        grid=(n // many,),
        in_specs=[
            pl.BlockSpec((many, 64, LANES), lambda i: (i, 0, 0)),
            pl.BlockSpec((9 * CH, many * LANES), lambda i: (0, i)),
            pl.BlockSpec((many, CH, 9 * LANES), lambda i: (i, 0, 0)),
        ]
        + [whole(a) for a in consts],
        out_specs=pl.BlockSpec((many, 48, LANES), lambda i: (i, 0, 0)),
        scratch=[
            pltpu.VMEM((128, LANES), f32),
            pltpu.VMEM((128, LANES), f32),
            pltpu.VMEM((16, EDGES), f32),
            pltpu.VMEM((3 * CH, EDGES), f32),
            pltpu.VMEM((CH, EDGES), f32),
            pltpu.VMEM((CH, 9 * LANES), f32),
            pltpu.VMEM((CH, 9 * LANES), f32),
            pltpu.VMEM((HID, EDGES), f32),
            pltpu.VMEM((HID, EDGES), f32),
            pltpu.VMEM((3 * CH, EDGES), bf16),
            pltpu.VMEM((128, LANES), f32),
            pltpu.VMEM((16, EDGES), f32),
            pltpu.VMEM((128, LANES), f32),
        ]
        * many,
        flops=n * 2000000000,
    )(geo, grad, keep, *consts)


def build_hot(vcol, b, hot, s):
    iota = lax.broadcasted_iota(jnp.int32, (COLS, LANES), 0)
    v = vcol[b, s : s + 1, :]
    hot[:, lanes(b * SLOTS + s)] = (iota == v).astype(f32).astype(bf16)


def layer_two_kernel(
    tl, tx, ty, geos, vcol, occ, first, second, third, third_t, second_t, first_t, mf, mb, of, ob,
    coef, lin, rh, rht, ro, energy, dl, dx_, dy_, dgeo,
    tab, yref, basrow, bas, wref, aref, dref, e1, e2, dwref, dyref, dbrow, dbas,
    hot, gat0, gat1, dgat,
):
    gats = (gat0, gat1, gat0)
    tab[:, 0:384] = tl[...]
    tab[:, 384:640] = tx[...]
    tab[:, 640:1408] = ty[...]
    dyref[...] = jnp.zeros_like(dyref)

    def gather(b, j):
        here = pl.ds(pl.multiple_of(j * 256, 256), 256)
        there = pl.ds(pl.multiple_of(b * EDGES + j * 256, 256), 256)
        gats[b][:, here] = mm(tab[...], hot[:, there]).astype(bf16)

    def messages(gat, c):
        acc = [None] * 9

        def add(k, v):
            acc[k] = v if acc[k] is None else acc[k] + v

        r = [pl.ds(pl.multiple_of(c * 16 + q * CH, 16), 16) for q in range(9)]
        for s in range(SLOTS):
            y = [yref[k * 16 + s : k * 16 + s + 1, :] for k in range(8)]
            x = [gat[r[q], lanes(s)].astype(f32) for q in range(9)]
            w = [wref[r[q], lanes(s)] for q in range(7)]
            a1 = sum_of([y[k] * x[k + 1] for k in range(3)])
            a2 = sum_of([y[k] * x[k + 1] for k in range(3, 8)])
            add(0, w[0] * x[0] + w[1] * a1 + w[2] * a2)
            t1, t2 = w[3] * x[0], w[5] * x[0]
            for k in range(8):
                add(k + 1, (t1 if k < 3 else t2) * y[k] + (w[4] if k < 3 else w[6]) * x[k + 1])
        for k in range(9):
            aref[r[0], lanes(k)] = acc[k] * (1.0 / SLOTS)

    def middle(b):
        mixed(mf, aref, dref)
        for r in ctiles():
            p = [dref[r, lanes(k)] for k in range(9)]
            c = [coef[r, k : k + 1] for k in range(3)]
            aref[r, lanes(0)] = (
                p[0]
                + c[0] * p[0] * p[0]
                + c[1] * sum_of([p[k] * p[k] for k in range(1, 4)])
                + c[2] * sum_of([p[k] * p[k] for k in range(4, 9)])
            )
        base = tab[0:CH, lanes(b)].astype(f32)
        scal = mm(of[...], split3(aref[:, lanes(0)])) + base
        h, e = silu_parts(mm(rht[...], split3(scal)))
        mask = occ[:, lanes(b)]
        tot = jnp.sum(ro[...] * h, axis=0, keepdims=True) + jnp.sum(lin[...] * base, axis=0, keepdims=True)
        energy[:, lanes(b)] = tot * mask
        ds = mm(rh[...], split3(ro[...] * e * mask))
        dl[0:CH, lanes(b)] = ds + lin[...] * mask
        aref[:, lanes(1)] = mm(ob[...], split3(ds * (1.0 / SLOTS)))
        for r in ctiles():
            db = aref[r, lanes(1)]
            c = [coef[r, k : k + 1] for k in range(3)]
            aref[r, lanes(0)] = db * (1.0 + 2.0 * c[0] * dref[r, lanes(0)])
            dp, dt = 2.0 * c[1] * db, 2.0 * c[2] * db
            for k in range(1, 9):
                aref[r, lanes(k)] = (dp if k < 4 else dt) * dref[r, lanes(k)]
        mixed(mb, aref, dref)

    def slot(gat, b, s):
        here = pl.ds(pl.multiple_of(s * LANES, LANES), LANES)
        there = pl.ds(pl.multiple_of(b * EDGES + s * LANES, LANES), LANES)
        y = [yref[pl.ds(k * 16 + s, 1), :] for k in range(8)]
        dy = [None] * 8
        for cc in range(CH // 16):
            r = [slice(q * CH + cc * 16, q * CH + cc * 16 + 16) for q in range(9)]
            x = [gat[r[q], here].astype(f32) for q in range(9)]
            w = [wref[r[q], here] for q in range(7)]
            d = [dref[r[0], lanes(k)] for k in range(9)]
            t1 = sum_of([y[k] * d[k + 1] for k in range(3)])
            t2 = sum_of([y[k] * d[k + 1] for k in range(3, 8)])
            a1 = sum_of([y[k] * x[k + 1] for k in range(3)])
            a2 = sum_of([y[k] * x[k + 1] for k in range(3, 8)])
            b1 = sum_of([d[k + 1] * x[k + 1] for k in range(3)])
            b2 = sum_of([d[k + 1] * x[k + 1] for k in range(3, 8)])
            dgat[r[0], there] = (w[0] * d[0] + w[3] * t1 + w[5] * t2).astype(bf16)
            m1, m2 = w[1] * d[0], w[2] * d[0]
            n1, n2 = w[3] * x[0], w[5] * x[0]
            for k in range(8):
                m, n, q = (m1, n1, w[4]) if k < 3 else (m2, n2, w[6])
                dgat[r[k + 1], there] = (m * y[k] + q * d[k + 1]).astype(bf16)
                v = m * x[k + 1] + n * d[k + 1]
                v = v[0:8] + v[8:16]
                dy[k] = v if dy[k] is None else dy[k] + v
            for q, v in enumerate((d[0] * x[0], d[0] * a1, d[0] * a2, x[0] * t1, b1, x[0] * t2, b2)):
                dwref[r[q], here] = v.astype(bf16)
        for k in range(8):
            dyref[pl.ds(k * 16 + s, 1), :] = jnp.sum(dy[k], axis=0, keepdims=True)

    def loop(n, *parts):
        def body(j, _):
            for part in parts:
                part(j)
            return 0

        lax.fori_loop(0, n, body, 0)

    for s in range(SLOTS):
        build_hot(vcol, 0, hot, s)
    geoms = [geometry(*(geos[b, k * 16 : k * 16 + 16, :] for k in range(3))) for b in range(LOCAL)]
    for b in range(LOCAL):
        gat = gats[b]
        place_geometry(geoms[b], yref, basrow, bas)
        radial_forward(bas, first, second, third, wref, e1, e2)
        if b == 0:
            for j in range(6):
                gather(0, j)
                for q in (2 * j, 2 * j + 1):
                    build_hot(vcol, 1, hot, q)
                    build_hot(vcol, 2, hot, q)
        loop(CH // 16, lambda c: messages(gat, c))
        middle(b)

        def slots(j):
            slot(gat, b, 2 * j)
            slot(gat, b, 2 * j + 1)

        if b + 1 < LOCAL:
            loop(6, slots, lambda j: gather(b + 1, j))
        else:
            loop(6, slots)
        radial_back(dwref, third_t, second_t, first_t, e1, e2, dbrow, dbas)
        gx, gy, gz = geometry_back(geoms[b], dyref, dbas)
        dgeo[b, 0:16, :] = gx
        dgeo[b, 16:32, :] = gy
        dgeo[b, 32:48, :] = gz
    for out, place, start, size in PIECES:
        out = (dl, dx_, dy_)[out]
        got = mm_nt(dgat[...], hot[start : start + size, :])
        here = slice(place, place + size)
        if out is dl:
            out[0:CH, here] = out[0:CH, here] + got[0:CH]
            out[CH:, here] = got[CH:]
        else:
            out[:, here] = got


PIECES = ((0, 0, 0, 256), (0, 256, 256, 128), (1, 0, 384, 256), (2, 0, 640, 256), (2, 256, 896, 256), (2, 512, 1152, 256))


def layer_two(tl, tx, ty, geo, vcol, occ, w):
    first, second, third = w["r2"]
    return call(
        layer_two_kernel,
        (shape(1, LOCAL * LANES), shape(9 * CH, 384), shape(9 * CH, 256), shape(9 * CH, 768), shape(LOCAL, 48, LANES)),
        scratch=[
            pltpu.VMEM((9 * CH, COLS), bf16),
            pltpu.VMEM((128, LANES), f32),
            pltpu.VMEM((128, LANES), f32),
            pltpu.VMEM((16, EDGES), f32),
            pltpu.VMEM((7 * CH, EDGES), f32),
            pltpu.VMEM((CH, 9 * LANES), f32),
            pltpu.VMEM((CH, 9 * LANES), f32),
            pltpu.VMEM((HID, EDGES), f32),
            pltpu.VMEM((HID, EDGES), f32),
            pltpu.VMEM((7 * CH, EDGES), bf16),
            pltpu.VMEM((128, LANES), f32),
            pltpu.VMEM((16, EDGES), f32),
            pltpu.VMEM((128, LANES), f32),
        ]
        + [pltpu.VMEM((COLS, 3 * EDGES), bf16)]
        + [pltpu.VMEM((9 * CH, EDGES), bf16)] * 2
        + [pltpu.VMEM((9 * CH, 3 * EDGES), bf16)],
        flops=40000000000,
    )(tl, tx, ty, geo, vcol, occ, first, second, third, *w["b2"], w["mf2"], w["mb2"], w["of2"],
      w["ob2"], w["coef2"], w["lin"], w["rh"], w["rht"], w["ro"])


def split_rows(x):
    hi = x.astype(bf16).astype(f32)
    rest = x - hi
    mid = rest.astype(bf16).astype(f32)
    return hi, mid, rest - mid


def place_border(x, border):
    slots = lax.broadcasted_iota(jnp.int32, (2 * LANES, LANES), 0)
    hot = (slots == border[...]).astype(f32).astype(bf16)
    n = x.shape[0]
    got = mm_nt(jnp.concatenate(split_rows(x), axis=0).astype(bf16), hot)
    return got[:n] + got[n : 2 * n] + got[2 * n :]


def columns_kernel(g2, g1, b0, b1, b2, b3, vcol, border, out, tot, lhs, hot):
    tot[...] = jnp.zeros_like(tot)
    for b in range(LOCAL):
        tot[b, 0:48, :] = g2[b] + g1[b]
    placed = place_border(b0[...] + b1[...] + (b2[...] + b3[...]), border)
    for b in range(2):
        tot[b, 0:48, :] = tot[b, 0:48, :] + placed[:, lanes(b)]
    iota = lax.broadcasted_iota(jnp.int32, (LANES, LANES), 0)
    total = jnp.zeros((16 * 11, LANES), f32)
    owns = []
    for b in range(LOCAL):
        own = jnp.zeros((4, LANES), f32)
        for s in range(SLOTS):
            x = tot[b, pl.ds(s, 4, stride=16), :]
            own = own + x
            hi, mid, lo = split_rows(x)
            part = jnp.concatenate([hi, mid, lo, jnp.zeros_like(x)], axis=0)
            v = vcol[b, s : s + 1, :]
            hot[:, lanes(s)] = (iota == (v & 127)).astype(f32).astype(bf16)
            block = v >> 7
            for k in range(11):
                lhs[k * 16 : k * 16 + 16, lanes(s)] = jnp.where(block == k, part, 0.0).astype(bf16)
        total = total + mm_nt(lhs[...], hot[...])
        owns.append(own)
    out[...] = jnp.zeros_like(out)
    for k in range(11):
        got = total[k * 16 : k * 16 + 4] + total[k * 16 + 4 : k * 16 + 8] + total[k * 16 + 8 : k * 16 + 12]
        out[0:4, lanes(k)] = got - owns[k] if k < LOCAL else got


def forces_kernel(col, r1, r2, xp, xn, border, out):
    total = xp[...] + xn[...] + (r1[:, lanes(1)] + r2[:, lanes(1)])
    placed = place_border(total, border)
    out[:, 0:256] = -(col[0:3, 0:256] + placed[0:3])
    out[:, 256:384] = -col[0:3, 256:384]


def from_behind(block, axis, distance):
    count = lax.axis_size(axis)
    route = [((i - distance) % count, i) for i in range(count)]
    return lax.ppermute(block, axis, route)


def eye(n):
    r = lax.broadcasted_iota(jnp.int32, (n, n), 0)
    return (r == lax.broadcasted_iota(jnp.int32, (n, n), 1)).astype(f32)


def turned(x):
    return lax.dot_general(
        eye(x.shape[1]), x, (((1,), (1,)), ((), ())), precision=lax.Precision.HIGHEST,
        preferred_element_type=f32,
    )


def left3(x):
    hi = x.astype(bf16).astype(f32)
    return jnp.concatenate([hi, hi, x - hi], axis=-1).astype(bf16)


def stacked(x):
    hi = x.astype(bf16).astype(f32)
    return jnp.concatenate([hi, x - hi], axis=0).astype(bf16)


def prepare_kernel(
    emb, rin, rmid, rout1, rout2, mix, mo1, mo2, c1, c2, lin, rh, ro,
    f1, s1, t1, f2, s2, t2, tt1, st1, ft1, tt2, st2, ft2, mf1, mb1, mf2, mb2, of1, ob1, of2, ob2,
    k1, k2, embo, lino, rho, rhto, roo, pad,
):
    for t, (f, s, o, tt, st, ft, out, mf, mb) in enumerate(
        ((f1, s1, t1, tt1, st1, ft1, rout1, mf1, mb1), (f2, s2, t2, tt2, st2, ft2, rout2, mf2, mb2))
    ):
        x = rin[t]
        hi = x.astype(bf16).astype(f32)
        top = turned(jnp.concatenate([hi, hi], axis=0))
        low = turned(jnp.concatenate([x - hi, jnp.zeros_like(x)], axis=0))
        f[...] = jnp.concatenate([top, low], axis=0).astype(bf16)
        s[...] = left3(turned(rmid[t]))
        for p in range(o.shape[0] // CH):
            o[p * CH : (p + 1) * CH, :] = left3(turned(out[:, lanes(p)]))
        tt[...] = stacked(out[...])
        st[...] = left3(rmid[t])
        ft[...] = left3(jnp.concatenate([x, jnp.zeros_like(x)], axis=0))
        for l in range(3):
            mf[l] = left3(turned(mix[t, l]))
            mb[l] = left3(mix[t, l])
    for l in range(3):
        of1[l] = left3(turned(mo1[l]))
        ob1[l] = left3(mo1[l])
    of2[...] = left3(turned(mo2[...]))
    ob2[...] = left3(mo2[...])
    k1[...] = turned(c1[...])
    k2[...] = turned(c2[...])
    pad[...] = jnp.zeros_like(pad)
    pad[0 : emb.shape[0], :] = emb[...]
    embo[...] = stacked(turned(pad[...]))
    lino[...] = turned(lin[...])
    rho[...] = left3(rh[...])
    rhto[...] = left3(turned(rh[...]))
    roo[...] = turned(ro[...])


def prepare(embedding, radial_in, radial_mid, outs, mix, mix_out_one, mix_out_two, product_one, product_two, read_lin, read_hidden, read_out):
    def half(*dims):
        return shape(*dims, kind=bf16)

    paths = [o.shape[1] for o in outs]
    small = lambda n: [half(128, 16), half(HID, 192), half(n, 192)]
    back = lambda n: [half(128, n), half(HID, 192), half(16, 192)]
    square = half(CH, 384)
    three = half(3, CH, 384)
    names = ("r1", "r2", "b1", "b2")
    shapes = small(paths[0]) + small(paths[1]) + back(paths[0]) + back(paths[1])
    shapes += [three] * 6 + [square] * 2
    shapes += [shape(CH, 5), shape(CH, 3), half(256, CH), shape(CH, 1), half(CH, 48), half(16, 384), shape(16, 1)]
    got = call(prepare_kernel, tuple(shapes), scratch=[pltpu.VMEM((CH, CH), f32)], flops=4000000000)(
        embedding, radial_in, radial_mid, *outs, mix, mix_out_one, mix_out_two, product_one,
        product_two, read_lin[None], read_hidden, read_out[None],
    )
    w = {n: tuple(got[3 * i : 3 * i + 3]) for i, n in enumerate(names)}
    rest = ("mf1", "mb1", "mf2", "mb2", "of1", "ob1", "of2", "ob2", "coef1", "coef2", "emb", "lin", "rh", "rht", "ro")
    w.update(zip(rest, got[12:]))
    return w


def on_device(
    positions, species, dest_key, send_list, send_count, border, neighbours, embedding, radial_in,
    radial_mid, radial_out_one, radial_out_two, mix, mix_out_one, mix_out_two, product_one,
    product_two, read_lin, read_hidden, read_out,
):
    pos = positions[0, 0]
    spec = species[0]
    key = dest_key[0]
    rows = border[0]
    nbr = neighbours[0, 0].T
    packet = call(
        packet_kernel,
        shape(8, 256),
        scratch=[pltpu.VMEM((8, 256), f32)],
        in_specs=[VMEM, VMEM, VMEM, VMEM, SMEM],
    )(pos, spec, send_list.reshape(1, LANES), rows, send_count.reshape(4))
    xp = from_behind(packet, "gx", 1)
    xn = from_behind(packet, "gx", -1)
    wide = jnp.concatenate([packet, xp[:, LANES:], xn[:, LANES:]], axis=1)
    yp = from_behind(wide, "gy", 1)
    yn = from_behind(wide, "gy", -1)
    w = prepare(embedding, radial_in, radial_mid, (radial_out_one, radial_out_two), mix, mix_out_one,
                mix_out_two, product_one, product_two, read_lin, read_hidden, read_out)
    geo, bgeo, vcol, kinds, occ = call(
        edges_kernel,
        (
            shape(LOCAL, 64, LANES),
            shape(64, LANES),
            shape(LOCAL, 16, LANES, kind=jnp.int32),
            shape(1, COLS),
            shape(1, LOCAL * LANES),
        ),
        scratch=[pltpu.VMEM((8, COLS), f32)],
    )(pos, spec, key, xp, xn, yp, yn, nbr, rows)
    gxp = from_behind(bgeo, "gx", 1)
    gxn = from_behind(bgeo, "gx", -1)
    tl, kl = layer_one(geo, kinds[:, :384], NL, w)
    three = jnp.stack([gxp, bgeo, gxn])
    gyp = from_behind(three, "gy", 1)
    gyn = from_behind(three, "gy", -1)
    geo_x = jnp.stack([gxp, gxn])
    tx, kx = layer_one(geo_x, kinds[:, 384:640], NX, w)
    geo_y = jnp.concatenate([gyp, gyn], axis=0)
    ty, ky = layer_one(geo_y, kinds[:, 640:], NY, w)
    energy, dl, dx, dy, g2 = layer_two(tl, tx, ty, geo, vcol, occ, w)
    dgy = layer_one_back(geo_y, dy, ky, NY, w)
    ry1 = from_behind(dgy[0:3], "gy", -1)
    ry2 = from_behind(dgy[3:6], "gy", 1)
    dgx = layer_one_back(geo_x, dx, kx, NX, w)
    rx1 = from_behind(dgx[0] + ry1[0] + ry2[0], "gx", -1)
    rx2 = from_behind(dgx[1] + ry1[2] + ry2[2], "gx", 1)
    g1 = layer_one_back(geo, dl, kl, NL, w)
    col = call(
        columns_kernel,
        shape(8, COLS),
        scratch=[
            pltpu.VMEM((LOCAL, 64, LANES), f32),
            pltpu.VMEM((11 * 16, EDGES), bf16),
            pltpu.VMEM((LANES, EDGES), bf16),
        ],
    )(g2, g1, ry1[1], ry2[1], rx1, rx2, vcol, rows)
    r1 = from_behind(col[:, 640:1024], "gy", -1)
    r2 = from_behind(col[:, 1024:1408], "gy", 1)
    sx1 = from_behind(col[:, 384:512] + r1[:, 0:128] + r2[:, 0:128], "gx", -1)
    sx2 = from_behind(col[:, 512:640] + r1[:, 256:384] + r2[:, 256:384], "gx", 1)
    forces = call(forces_kernel, shape(3, LOCAL * LANES))(col, r1, r2, sx1, sx2, rows)
    return energy[None], forces[None, None]


def solution(mesh):
    along = P("gx", "gy")
    in_specs = (along,) * 7 + (P(),) * 13
    return jax.shard_map(
        on_device, mesh=mesh, in_specs=in_specs, out_specs=(along, along), check_vma=False
    )
```

```python
import functools
import math

import jax
import jax.numpy as jnp
from jax import lax
from jax.experimental import pallas as pl
from jax.experimental.pallas import tpu as pltpu
from jax.sharding import PartitionSpec as P

f32 = jnp.float32
bf16 = jnp.bfloat16
CH = 128
HID = 64
SLOTS = 12
LANES = 128
EDGES = SLOTS * LANES
LOCAL = 3
COLS = 11 * LANES
NL, NX, NY = 1, 2, 2
RADIUS = 5.0
SCALE = math.sqrt(2.0 / RADIUS)
R3 = math.sqrt(3.0)
R5 = math.sqrt(5.0)
R15 = math.sqrt(15.0)
VMEM = pl.BlockSpec(memory_space=pltpu.VMEM)
SMEM = pl.BlockSpec(memory_space=pltpu.SMEM)
LIMIT = 60 * 1024 * 1024


def call(kernel, out_shape, scratch=(), flops=1000000, in_specs=None, **kw):
    return pl.pallas_call(
        kernel,
        out_shape=out_shape,
        scratch_shapes=list(scratch),
        compiler_params=pltpu.CompilerParams(vmem_limit_bytes=LIMIT),
        cost_estimate=pl.CostEstimate(flops=flops, bytes_accessed=1000000, transcendentals=0),
        **({"in_specs": in_specs} if in_specs is not None else {}),
        **kw,
    )


def shape(*dims, kind=f32):
    return jax.ShapeDtypeStruct(dims, kind)


def lanes(i, n=1):
    return slice(i * LANES, (i + n) * LANES)


def hi_lo(x):
    hi = x.astype(bf16)
    return hi, (x - hi.astype(f32)).astype(bf16)


def split3(x):
    hi, lo = hi_lo(x)
    return jnp.concatenate([hi, lo, hi], axis=0)


def mm(a, b):
    return jnp.dot(a, b, preferred_element_type=f32)


def mm_nt(a, b):
    return lax.dot_general(a, b, (((1,), (1,)), ((), ())), preferred_element_type=f32)


def silu_parts(x):
    s = 0.5 * jnp.tanh(0.5 * x) + 0.5
    h = x * s
    return h, s + h * (1.0 - s)


def take_lanes(chunk, index):
    return jnp.take_along_axis(chunk, index, axis=1, mode="promise_in_bounds")


def gather_columns(ref, rows, index, chunks):
    low = index & 127
    block = index >> 7
    out = take_lanes(ref[rows, lanes(0)], low)
    for c in range(1, chunks):
        out = jnp.where(block == c, take_lanes(ref[rows, lanes(c)], low), out)
    return out


def packet_kernel(pos, spec, listed, border, count, out, tbl):
    tbl[...] = jnp.zeros_like(tbl)
    tbl[0:3, :] = pos[...]
    tbl[3:4, :] = spec[...].astype(f32)
    row = lax.broadcasted_iota(jnp.int32, (8, LANES), 0)
    lane = lax.broadcasted_iota(jnp.int32, (8, LANES), 1)
    way = lane >> 5
    index = jnp.broadcast_to(listed[...], (8, LANES))
    got = gather_columns(tbl, slice(0, 8), index, 2)
    amount = jnp.where(way == 0, count[0], jnp.where(way == 1, count[1], jnp.where(way == 2, count[2], count[3])))
    step = jnp.where((way & 1) == 0, -1.0, 1.0).astype(f32)
    got = got + jnp.where(row == (way >> 1), step, 0.0)
    got = jnp.where((row == 3) & ((lane & 31) >= amount), -1.0, got)
    out[:, lanes(0)] = got
    out[:, lanes(1)] = gather_columns(tbl, slice(0, 8), jnp.broadcast_to(border[...], (8, LANES)), 2)


PLACE = {1: 3, 7: 4, 0: 5, 3: 6, 6: 7, 2: 8, 5: 9, 8: 10}


def edges_kernel(pos, spec, key, xp, xn, yp, yn, nbr, border, geo, bgeo, vcol, kinds, occ, tbl):
    tbl[...] = jnp.zeros_like(tbl)
    tbl[0:3, 0:256] = pos[...]
    tbl[3:4, 0:256] = spec[...].astype(f32)
    tbl[4:5, 0:256] = (key[...] == 0).astype(f32)
    row = lax.broadcasted_iota(jnp.int32, (8, LANES), 0)
    way = lax.broadcasted_iota(jnp.int32, (8, LANES), 1) >> 5
    came = jnp.where(
        way == 0,
        xp[:, lanes(0)],
        jnp.where(way == 1, xn[:, lanes(0)], jnp.where(way == 2, yp[:, lanes(0)], yn[:, lanes(0)])),
    )
    tbl[:, lanes(2)] = came
    tbl[4:5, lanes(2)] = (came[3:4] >= 0).astype(f32)

    def ghost(place, block, dx, dy):
        moved = block + jnp.where(row == 0, dx, jnp.where(row == 1, dy, jnp.where(row == 4, 1.0, 0.0)))
        tbl[:, lanes(place)] = moved

    ghost(3, xp[:, lanes(1)], -1.0, 0.0)
    ghost(4, xn[:, lanes(1)], 1.0, 0.0)
    for base, got, dy in ((5, yp, -1.0), (8, yn, 1.0)):
        ghost(base, got[:, lanes(2)], -1.0, dy)
        ghost(base + 1, got[:, lanes(1)], 0.0, dy)
        ghost(base + 2, got[:, lanes(3)], 1.0, dy)
    kinds[...] = jnp.maximum(tbl[3:4, :], 0.0)
    occ[...] = tbl[4:5, 0 : LOCAL * LANES]
    geo[...] = jnp.zeros_like(geo)
    vcol[...] = jnp.full_like(vcol, -1)
    for b in range(LOCAL):
        own = tbl[:, lanes(b)]
        for s in range(SLOTS):
            n = nbr[s : s + 1, lanes(b)]
            old = n >> 7
            block = jnp.minimum(old, 2)
            for was, now in PLACE.items():
                block = jnp.where(old == was + 3, now, block)
            col = jnp.maximum(block, 0) * 128 + (n & 127)
            got = gather_columns(tbl, slice(0, 8), jnp.broadcast_to(col, (8, LANES)), 11)
            valid = (n >= 0) & (got[4:5] > 0.5) & (own[4:5] > 0.5)
            off = got - own
            val = jnp.where(row < 3, off, jnp.where(jnp.broadcast_to(valid, (8, LANES)), got, -1.0))
            geo[b, pl.ds(s, 4, stride=16), :] = val[0:4]
            vcol[b, s : s + 1, :] = jnp.where(valid, col, -1)
    index = jnp.broadcast_to(border[...], (8, LANES))
    low = index & 127
    for t in range(8):
        rows = slice(t * 8, t * 8 + 8)
        bgeo[rows, :] = jnp.where(
            (index >> 7) == 0, take_lanes(geo[0, rows, :], low), take_lanes(geo[1, rows, :], low)
        )


def geometry(ox, oy, oz):
    d = jnp.sqrt(ox * ox + oy * oy + oz * oz + 1.0)
    rd = 1.0 / d
    u = (ox * rd, oy * rd, oz * rd)
    t = d * (1.0 / RADIUS)
    t2 = t * t
    t5 = t2 * t2 * t
    t6 = t5 * t
    env = 1.0 - 28.0 * t6 + 48.0 * t6 * t - 21.0 * t6 * t2
    theta = (math.pi / RADIUS) * d
    s1, c1 = jnp.sin(theta), jnp.cos(theta)
    sines, cosines = [s1], [c1]
    before_s, before_c = jnp.zeros_like(s1), jnp.ones_like(c1)
    for _ in range(7):
        ns = 2.0 * c1 * sines[-1] - before_s
        nc = 2.0 * c1 * cosines[-1] - before_c
        before_s, before_c = sines[-1], cosines[-1]
        sines.append(ns)
        cosines.append(nc)
    slope = (-168.0 * t5 + 336.0 * t6 - 168.0 * t6 * t) * (1.0 / RADIUS)
    return u, d, rd, env, slope, sines, cosines


def harmonics(u):
    x, y, z = u
    return [
        R3 * x,
        R3 * y,
        R3 * z,
        R15 * x * y,
        R15 * y * z,
        0.5 * R5 * (2.0 * z * z - x * x - y * y),
        R15 * x * z,
        0.5 * R15 * (x * x - y * y),
    ]


def place_geometry(geo, yref, basrow, bas):
    u, d, rd, env, slope, sines, cosines = geo
    for k, h in enumerate(harmonics(u)):
        yref[k * 16 : k * 16 + 16, :] = h
    factor = SCALE * env * rd
    for m in range(8):
        basrow[m * 16 : m * 16 + 16, :] = sines[m] * factor
    for s in range(SLOTS):
        got = basrow[pl.ds(s, 8, stride=16), :]
        bas[0:8, lanes(s)] = got
        bas[8:16, lanes(s)] = got - got.astype(bf16).astype(f32)


def geometry_back(geo, dyref, dbas):
    (x, y, z), d, rd, env, slope, sines, cosines = geo
    g = [dyref[k * 16 : k * 16 + 16, :] for k in range(8)]
    dx = R3 * g[0] + R15 * (y * g[3] + z * g[6] + x * g[7]) - R5 * x * g[5]
    dy = R3 * g[1] + R15 * (x * g[3] + z * g[4] - y * g[7]) - R5 * y * g[5]
    dz = R3 * g[2] + R15 * (y * g[4] + x * g[6]) + 2.0 * R5 * z * g[5]
    along = jnp.zeros_like(x)
    turned = jnp.zeros_like(x)
    for m in range(8):
        db = dbas[m * 16 : m * 16 + 16, :]
        along = along + db * sines[m]
        turned = turned + ((m + 1) * math.pi / RADIUS) * db * cosines[m]
    dd = SCALE * rd * (turned * env + along * (slope - env * rd))
    dd = dd - (dx * x + dy * y + dz * z) * rd
    return dx * rd + x * dd, dy * rd + y * dd, dz * rd + z * dd


def radial_forward(bas, first, second, third, wref, e1=None, e2=None):
    pre = mm(first[...], bas[...].astype(bf16))
    h, e = silu_parts(pre[:HID] + pre[HID:])
    if e1 is not None:
        e1[...] = e
    h, e = silu_parts(mm(second[...], split3(h)))
    if e2 is not None:
        e2[...] = e
    h = split3(h)
    for p in range(third.shape[0] // CH):
        wref[p * CH : (p + 1) * CH, :] = mm(third[p * CH : (p + 1) * CH, :], h)


def radial_back(dwref, third_t, second_t, first_t, e1, e2, dbrow, dbas):
    both = mm(third_t[...], dwref[...])
    dp = (both[:HID] + both[HID:]) * e2[...]
    dp = mm(second_t[...], split3(dp)) * e1[...]
    dbrow[...] = mm(first_t[...], split3(dp))
    dbas[...] = jnp.zeros_like(dbas)
    for s in range(SLOTS):
        dbas[pl.ds(s, 8, stride=16), :] = dbrow[0:8, lanes(s)]


ORDERS = ((0, 1), (1, 3), (4, 5))


def mixed(matrices, values, out):
    for l, (start, n) in enumerate(ORDERS):
        out[:, lanes(start, n)] = mm(matrices[l], split3(values[:, lanes(start, n)]))


def sum_of(terms):
    total = terms[0]
    for t in terms[1:]:
        total = total + t
    return total


def first_features(geo, emb, fref):
    iota = lax.broadcasted_iota(jnp.int32, (CH, LANES), 0)
    for s in range(SLOTS):
        kind = geo[48 + s : 49 + s, :].astype(jnp.int32)
        hot = (iota == kind).astype(f32).astype(bf16)
        both = mm(emb[...], hot)
        fref[:, lanes(s)] = both[:CH] + both[CH:]


def ctiles():
    return [slice(c * 16, c * 16 + 16) for c in range(CH // 16)]


def layer_one_kernel(many, geos, kinds, first, second, third, emb, mf, mo, coef, out, keeps, *scratch):
    sets = [scratch[6 * q : 6 * q + 6] for q in range(many)]
    for q, (yref, basrow, bas, wref, fref, aref) in enumerate(sets):
        geo = geos.at[q]
        place_geometry(geometry(geo[0:16, :], geo[16:32, :], geo[32:48, :]), yref, basrow, bas)
    for q, (yref, basrow, bas, wref, fref, aref) in enumerate(sets):
        radial_forward(bas, first, second, third, wref)
        first_features(geos.at[q], emb, fref)

    def messages(c, _):
        r0 = pl.ds(pl.multiple_of(c * 16, 16), 16)
        r1 = pl.ds(pl.multiple_of(c * 16 + CH, 16), 16)
        r2 = pl.ds(pl.multiple_of(c * 16 + 2 * CH, 16), 16)
        for yref, basrow, bas, wref, fref, aref in sets:
            acc = [None] * 9

            def add(k, v):
                acc[k] = v if acc[k] is None else acc[k] + v

            for s in range(SLOTS):
                f = fref[r0, lanes(s)]
                add(0, wref[r0, lanes(s)] * f)
                w1 = wref[r1, lanes(s)] * f
                w2 = wref[r2, lanes(s)] * f
                for k in range(8):
                    add(k + 1, (w1 if k < 3 else w2) * yref[k * 16 + s : k * 16 + s + 1, :])
            for k in range(9):
                aref[r0, lanes(k)] = acc[k] * (1.0 / SLOTS)
        return 0

    lax.fori_loop(0, CH // 16, messages, 0, unroll=True)
    for q in range(many):
        mixed(mf, sets[q][5], keeps.at[q])
    for q in range(many):
        keep, aref = keeps.at[q], sets[q][5]
        for r in ctiles():
            p = [keep[r, lanes(k)] for k in range(9)]
            c = [coef[r, k : k + 1] for k in range(5)]
            aref[r, lanes(0)] = (
                p[0]
                + c[0] * p[0] * p[0]
                + c[1] * sum_of([p[k] * p[k] for k in range(1, 4)])
                + c[2] * sum_of([p[k] * p[k] for k in range(4, 9)])
            )
            up, ut = 1.0 + c[3] * p[0], 1.0 + c[4] * p[0]
            for k in range(1, 9):
                aref[r, lanes(k)] = p[k] * (up if k < 4 else ut)
    iota = lax.broadcasted_iota(jnp.int32, (CH, LANES), 0)
    for q in range(many):
        aref = sets[q][5]
        hot = (iota == kinds[:, lanes(q)].astype(jnp.int32)).astype(f32).astype(bf16)
        both = mm(emb[...], hot)
        out[0:CH, lanes(q)] = (mm(mo[0], split3(aref[:, lanes(0)])) + (both[:CH] + both[CH:])).astype(bf16)
        for l, (start, n) in enumerate(ORDERS[1:], 1):
            got = mm(mo[l], split3(aref[:, lanes(start, n)]))
            for k in range(n):
                out[(start + k) * CH : (start + k + 1) * CH, lanes(q)] = got[:, lanes(k)].astype(bf16)


def whole(a):
    rank = len(a.shape)
    return pl.BlockSpec(a.shape, lambda i: (0,) * rank)


def layer_one(geo, kinds, many, weights):
    n = geo.shape[0]
    first, second, third = weights["r1"]
    consts = (first, second, third, weights["emb"], weights["mf1"], weights["of1"], weights["coef1"])
    return call(
        functools.partial(layer_one_kernel, many),
        (shape(9 * CH, n * LANES, kind=bf16), shape(n, CH, 9 * LANES)),
        grid=(n // many,),
        in_specs=[
            pl.BlockSpec((many, 64, LANES), lambda i: (i, 0, 0)),
            pl.BlockSpec((1, many * LANES), lambda i: (0, i)),
        ]
        + [whole(a) for a in consts],
        out_specs=(
            pl.BlockSpec((9 * CH, many * LANES), lambda i: (0, i)),
            pl.BlockSpec((many, CH, 9 * LANES), lambda i: (i, 0, 0)),
        ),
        scratch=[
            pltpu.VMEM((128, LANES), f32),
            pltpu.VMEM((128, LANES), f32),
            pltpu.VMEM((16, EDGES), f32),
            pltpu.VMEM((3 * CH, EDGES), f32),
            pltpu.VMEM((CH, EDGES), f32),
            pltpu.VMEM((CH, 9 * LANES), f32),
        ]
        * many,
        flops=n * 900000000,
    )(geo, kinds, *consts)


def layer_one_back_kernel(
    many, geos, grad, keeps, first, second, third, third_t, second_t, first_t, emb, mb, mo, coef, out, *scratch
):
    sets = [scratch[13 * q : 13 * q + 13] for q in range(many)]
    geoms = []
    for q in range(many):
        geo, (yref, basrow, bas) = geos.at[q], sets[q][:3]
        geoms.append(geometry(geo[0:16, :], geo[16:32, :], geo[32:48, :]))
        place_geometry(geoms[q], yref, basrow, bas)
    for q in range(many):
        yref, basrow, bas, wref, fref, aref, dref, e1, e2, dwref, dyref, dbrow, dbas = sets[q]
        radial_forward(bas, first, second, third, wref, e1, e2)
        first_features(geos.at[q], emb, fref)
    for q in range(many):
        aref, dref = sets[q][5:7]
        for k in range(9):
            aref[:, lanes(k)] = grad[k * CH : (k + 1) * CH, lanes(q)]
        mixed(mo, aref, dref)
    for q in range(many):
        aref, dref = sets[q][5:7]
        keep = keeps.at[q]
        for r in ctiles():
            p = [keep[r, lanes(k)] for k in range(9)]
            g = [dref[r, lanes(k)] for k in range(9)]
            c = [coef[r, k : k + 1] for k in range(5)]
            aref[r, lanes(0)] = (1.0 / SLOTS) * (
                g[0] * (1.0 + 2.0 * c[0] * p[0])
                + c[3] * sum_of([p[k] * g[k] for k in range(1, 4)])
                + c[4] * sum_of([p[k] * g[k] for k in range(4, 9)])
            )
            g = [v * (1.0 / SLOTS) for v in g]
            up, ut = 1.0 + c[3] * p[0], 1.0 + c[4] * p[0]
            vp, vt = 2.0 * c[1] * g[0], 2.0 * c[2] * g[0]
            for k in range(1, 9):
                aref[r, lanes(k)] = g[k] * (up if k < 4 else ut) + p[k] * (vp if k < 4 else vt)
    for q in range(many):
        mixed(mb, *sets[q][5:7])
        sets[q][10][...] = jnp.zeros_like(sets[q][10])

    def slot(s, _):
        here = pl.ds(pl.multiple_of(s * LANES, LANES), LANES)
        for yref, basrow, bas, wref, fref, aref, dref, e1, e2, dwref, dyref, dbrow, dbas in sets:
            y = [yref[pl.ds(k * 16 + s, 1), :] for k in range(8)]
            dy = [None] * 8
            for c in range(CH // 16):
                r0, r1, r2 = (slice(q * CH + c * 16, q * CH + c * 16 + 16) for q in range(3))
                f = fref[r0, here]
                w1 = wref[r1, here] * f
                w2 = wref[r2, here] * f
                d = [dref[r0, lanes(k)] for k in range(9)]
                dwref[r0, here] = (d[0] * f).astype(bf16)
                dwref[r1, here] = (f * sum_of([d[k + 1] * y[k] for k in range(3)])).astype(bf16)
                dwref[r2, here] = (f * sum_of([d[k + 1] * y[k] for k in range(3, 8)])).astype(bf16)
                for k in range(8):
                    v = (w1 if k < 3 else w2) * d[k + 1]
                    v = v[0:8] + v[8:16]
                    dy[k] = v if dy[k] is None else dy[k] + v
            for k in range(8):
                dyref[pl.ds(k * 16 + s, 1), :] = jnp.sum(dy[k], axis=0, keepdims=True)
        return 0

    lax.fori_loop(0, SLOTS, slot, 0, unroll=True)
    for yref, basrow, bas, wref, fref, aref, dref, e1, e2, dwref, dyref, dbrow, dbas in sets:
        radial_back(dwref, third_t, second_t, first_t, e1, e2, dbrow, dbas)
    for q in range(many):
        dx, dy, dz = geometry_back(geoms[q], sets[q][10], sets[q][12])
        out[q, 0:16, :] = dx
        out[q, 16:32, :] = dy
        out[q, 32:48, :] = dz


def layer_one_back(geo, grad, keep, many, weights):
    n = geo.shape[0]
    first, second, third = weights["r1"]
    consts = (first, second, third) + weights["b1"] + (
        weights["emb"], weights["mb1"], weights["ob1"], weights["coef1"])
    return call(
        functools.partial(layer_one_back_kernel, many),
        shape(n, 48, LANES),
        grid=(n // many,),
        in_specs=[
            pl.BlockSpec((many, 64, LANES), lambda i: (i, 0, 0)),
            pl.BlockSpec((9 * CH, many * LANES), lambda i: (0, i)),
            pl.BlockSpec((many, CH, 9 * LANES), lambda i: (i, 0, 0)),
        ]
        + [whole(a) for a in consts],
        out_specs=pl.BlockSpec((many, 48, LANES), lambda i: (i, 0, 0)),
        scratch=[
            pltpu.VMEM((128, LANES), f32),
            pltpu.VMEM((128, LANES), f32),
            pltpu.VMEM((16, EDGES), f32),
            pltpu.VMEM((3 * CH, EDGES), f32),
            pltpu.VMEM((CH, EDGES), f32),
            pltpu.VMEM((CH, 9 * LANES), f32),
            pltpu.VMEM((CH, 9 * LANES), f32),
            pltpu.VMEM((HID, EDGES), f32),
            pltpu.VMEM((HID, EDGES), f32),
            pltpu.VMEM((3 * CH, EDGES), bf16),
            pltpu.VMEM((128, LANES), f32),
            pltpu.VMEM((16, EDGES), f32),
            pltpu.VMEM((128, LANES), f32),
        ]
        * many,
        flops=n * 2000000000,
    )(geo, grad, keep, *consts)


def build_hot(vcol, b, hot, s):
    iota = lax.broadcasted_iota(jnp.int32, (COLS, LANES), 0)
    v = vcol[b, s : s + 1, :]
    hot[:, lanes(b * SLOTS + s)] = (iota == v).astype(f32).astype(bf16)


def layer_two_kernel(
    tl, tx, ty, geos, vcol, occ, first, second, third, third_t, second_t, first_t, mf, mb, of, ob,
    coef, lin, rh, rht, ro, energy, dl, dx_, dy_, dgeo,
    tab, yref, basrow, bas, wref, aref, dref, e1, e2, dwref, dyref, dbrow, dbas,
    hot, gat0, gat1, dgat,
):
    gats = (gat0, gat1, gat0)
    tab[:, 0:384] = tl[...]
    tab[:, 384:640] = tx[...]
    tab[:, 640:1408] = ty[...]
    dyref[...] = jnp.zeros_like(dyref)

    def gather(b, j):
        here = pl.ds(pl.multiple_of(j * 256, 256), 256)
        there = pl.ds(pl.multiple_of(b * EDGES + j * 256, 256), 256)
        gats[b][:, here] = mm(tab[...], hot[:, there]).astype(bf16)

    def messages(gat, c):
        acc = [None] * 9

        def add(k, v):
            acc[k] = v if acc[k] is None else acc[k] + v

        r = [pl.ds(pl.multiple_of(c * 16 + q * CH, 16), 16) for q in range(9)]
        for s in range(SLOTS):
            y = [yref[k * 16 + s : k * 16 + s + 1, :] for k in range(8)]
            x = [gat[r[q], lanes(s)].astype(f32) for q in range(9)]
            w = [wref[r[q], lanes(s)] for q in range(7)]
            a1 = sum_of([y[k] * x[k + 1] for k in range(3)])
            a2 = sum_of([y[k] * x[k + 1] for k in range(3, 8)])
            add(0, w[0] * x[0] + w[1] * a1 + w[2] * a2)
            t1, t2 = w[3] * x[0], w[5] * x[0]
            for k in range(8):
                add(k + 1, (t1 if k < 3 else t2) * y[k] + (w[4] if k < 3 else w[6]) * x[k + 1])
        for k in range(9):
            aref[r[0], lanes(k)] = acc[k] * (1.0 / SLOTS)

    def middle(b):
        mixed(mf, aref, dref)
        for r in ctiles():
            p = [dref[r, lanes(k)] for k in range(9)]
            c = [coef[r, k : k + 1] for k in range(3)]
            aref[r, lanes(0)] = (
                p[0]
                + c[0] * p[0] * p[0]
                + c[1] * sum_of([p[k] * p[k] for k in range(1, 4)])
                + c[2] * sum_of([p[k] * p[k] for k in range(4, 9)])
            )
        base = tab[0:CH, lanes(b)].astype(f32)
        scal = mm(of[...], split3(aref[:, lanes(0)])) + base
        h, e = silu_parts(mm(rht[...], split3(scal)))
        mask = occ[:, lanes(b)]
        tot = jnp.sum(ro[...] * h, axis=0, keepdims=True) + jnp.sum(lin[...] * base, axis=0, keepdims=True)
        energy[:, lanes(b)] = tot * mask
        ds = mm(rh[...], split3(ro[...] * e * mask))
        dl[0:CH, lanes(b)] = ds + lin[...] * mask
        aref[:, lanes(1)] = mm(ob[...], split3(ds * (1.0 / SLOTS)))
        for r in ctiles():
            db = aref[r, lanes(1)]
            c = [coef[r, k : k + 1] for k in range(3)]
            aref[r, lanes(0)] = db * (1.0 + 2.0 * c[0] * dref[r, lanes(0)])
            dp, dt = 2.0 * c[1] * db, 2.0 * c[2] * db
            for k in range(1, 9):
                aref[r, lanes(k)] = (dp if k < 4 else dt) * dref[r, lanes(k)]
        mixed(mb, aref, dref)

    def slot(gat, b, s):
        here = pl.ds(pl.multiple_of(s * LANES, LANES), LANES)
        there = pl.ds(pl.multiple_of(b * EDGES + s * LANES, LANES), LANES)
        y = [yref[pl.ds(k * 16 + s, 1), :] for k in range(8)]
        dy = [None] * 8
        for cc in range(CH // 16):
            r = [slice(q * CH + cc * 16, q * CH + cc * 16 + 16) for q in range(9)]
            x = [gat[r[q], here].astype(f32) for q in range(9)]
            w = [wref[r[q], here] for q in range(7)]
            d = [dref[r[0], lanes(k)] for k in range(9)]
            t1 = sum_of([y[k] * d[k + 1] for k in range(3)])
            t2 = sum_of([y[k] * d[k + 1] for k in range(3, 8)])
            a1 = sum_of([y[k] * x[k + 1] for k in range(3)])
            a2 = sum_of([y[k] * x[k + 1] for k in range(3, 8)])
            b1 = sum_of([d[k + 1] * x[k + 1] for k in range(3)])
            b2 = sum_of([d[k + 1] * x[k + 1] for k in range(3, 8)])
            dgat[r[0], there] = (w[0] * d[0] + w[3] * t1 + w[5] * t2).astype(bf16)
            m1, m2 = w[1] * d[0], w[2] * d[0]
            n1, n2 = w[3] * x[0], w[5] * x[0]
            for k in range(8):
                m, n, q = (m1, n1, w[4]) if k < 3 else (m2, n2, w[6])
                dgat[r[k + 1], there] = (m * y[k] + q * d[k + 1]).astype(bf16)
                v = m * x[k + 1] + n * d[k + 1]
                v = v[0:8] + v[8:16]
                dy[k] = v if dy[k] is None else dy[k] + v
            for q, v in enumerate((d[0] * x[0], d[0] * a1, d[0] * a2, x[0] * t1, b1, x[0] * t2, b2)):
                dwref[r[q], here] = v.astype(bf16)
        for k in range(8):
            dyref[pl.ds(k * 16 + s, 1), :] = jnp.sum(dy[k], axis=0, keepdims=True)

    def loop(n, *parts):
        def body(j, _):
            for part in parts:
                part(j)
            return 0

        lax.fori_loop(0, n, body, 0)

    for s in range(SLOTS):
        build_hot(vcol, 0, hot, s)
    geoms = [geometry(*(geos[b, k * 16 : k * 16 + 16, :] for k in range(3))) for b in range(LOCAL)]
    for b in range(LOCAL):
        gat = gats[b]
        place_geometry(geoms[b], yref, basrow, bas)
        radial_forward(bas, first, second, third, wref, e1, e2)
        if b == 0:
            for j in range(6):
                gather(0, j)
                for q in (2 * j, 2 * j + 1):
                    build_hot(vcol, 1, hot, q)
                    build_hot(vcol, 2, hot, q)
        loop(CH // 16, lambda c: messages(gat, c))
        middle(b)

        def slots(j):
            slot(gat, b, 2 * j)
            slot(gat, b, 2 * j + 1)

        if b + 1 < LOCAL:
            loop(6, slots, lambda j: gather(b + 1, j))
        else:
            loop(6, slots)
        radial_back(dwref, third_t, second_t, first_t, e1, e2, dbrow, dbas)
        gx, gy, gz = geometry_back(geoms[b], dyref, dbas)
        dgeo[b, 0:16, :] = gx
        dgeo[b, 16:32, :] = gy
        dgeo[b, 32:48, :] = gz
    def ghosts(j):
        here = pl.ds(pl.multiple_of(j * 256, 256), 256)
        dy_[:, here] = mm_nt(dgat[...], hot[pl.ds(pl.multiple_of(640 + j * 256, 128), 256), :])

    loop(3, ghosts)
    for out, place, start, size in PIECES:
        out = (dl, dx_, dy_)[out]
        got = mm_nt(dgat[...], hot[start : start + size, :])
        here = slice(place, place + size)
        if out is dl:
            out[0:CH, here] = out[0:CH, here] + got[0:CH]
            out[CH:, here] = got[CH:]
        else:
            out[:, here] = got


PIECES = ((0, 0, 0, 256), (0, 256, 256, 128), (1, 0, 384, 256))


def layer_two(tl, tx, ty, geo, vcol, occ, w):
    first, second, third = w["r2"]
    return call(
        layer_two_kernel,
        (shape(1, LOCAL * LANES), shape(9 * CH, 384), shape(9 * CH, 256), shape(9 * CH, 768), shape(LOCAL, 48, LANES)),
        scratch=[
            pltpu.VMEM((9 * CH, COLS), bf16),
            pltpu.VMEM((128, LANES), f32),
            pltpu.VMEM((128, LANES), f32),
            pltpu.VMEM((16, EDGES), f32),
            pltpu.VMEM((7 * CH, EDGES), f32),
            pltpu.VMEM((CH, 9 * LANES), f32),
            pltpu.VMEM((CH, 9 * LANES), f32),
            pltpu.VMEM((HID, EDGES), f32),
            pltpu.VMEM((HID, EDGES), f32),
            pltpu.VMEM((7 * CH, EDGES), bf16),
            pltpu.VMEM((128, LANES), f32),
            pltpu.VMEM((16, EDGES), f32),
            pltpu.VMEM((128, LANES), f32),
        ]
        + [pltpu.VMEM((COLS, 3 * EDGES), bf16)]
        + [pltpu.VMEM((9 * CH, EDGES), bf16)] * 2
        + [pltpu.VMEM((9 * CH, 3 * EDGES), bf16)],
        flops=40000000000,
    )(tl, tx, ty, geo, vcol, occ, first, second, third, *w["b2"], w["mf2"], w["mb2"], w["of2"],
      w["ob2"], w["coef2"], w["lin"], w["rh"], w["rht"], w["ro"])


def split_rows(x):
    hi = x.astype(bf16).astype(f32)
    rest = x - hi
    mid = rest.astype(bf16).astype(f32)
    return hi, mid, rest - mid


def place_border(x, border):
    slots = lax.broadcasted_iota(jnp.int32, (2 * LANES, LANES), 0)
    hot = (slots == border[...]).astype(f32).astype(bf16)
    n = x.shape[0]
    got = mm_nt(jnp.concatenate(split_rows(x), axis=0).astype(bf16), hot)
    return got[:n] + got[n : 2 * n] + got[2 * n :]


def columns_kernel(g2, g1, b0, b1, b2, b3, vcol, border, out, tot, lhs, hot):
    tot[...] = jnp.zeros_like(tot)
    for b in range(LOCAL):
        tot[b, 0:48, :] = g2[b] + g1[b]
    placed = place_border(b0[...] + b1[...] + (b2[...] + b3[...]), border)
    for b in range(2):
        tot[b, 0:48, :] = tot[b, 0:48, :] + placed[:, lanes(b)]
    iota = lax.broadcasted_iota(jnp.int32, (LANES, LANES), 0)
    total = jnp.zeros((16 * 11, LANES), f32)
    owns = []
    for b in range(LOCAL):
        own = jnp.zeros((4, LANES), f32)
        for s in range(SLOTS):
            x = tot[b, pl.ds(s, 4, stride=16), :]
            own = own + x
            hi, mid, lo = split_rows(x)
            part = jnp.concatenate([hi, mid, lo, jnp.zeros_like(x)], axis=0)
            v = vcol[b, s : s + 1, :]
            hot[:, lanes(s)] = (iota == (v & 127)).astype(f32).astype(bf16)
            block = v >> 7
            for k in range(11):
                lhs[k * 16 : k * 16 + 16, lanes(s)] = jnp.where(block == k, part, 0.0).astype(bf16)
        total = total + mm_nt(lhs[...], hot[...])
        owns.append(own)
    out[...] = jnp.zeros_like(out)
    for k in range(11):
        got = total[k * 16 : k * 16 + 4] + total[k * 16 + 4 : k * 16 + 8] + total[k * 16 + 8 : k * 16 + 12]
        out[0:4, lanes(k)] = got - owns[k] if k < LOCAL else got


def forces_kernel(col, r1, r2, xp, xn, border, out):
    total = xp[...] + xn[...] + (r1[:, lanes(1)] + r2[:, lanes(1)])
    placed = place_border(total, border)
    out[:, 0:256] = -(col[0:3, 0:256] + placed[0:3])
    out[:, 256:384] = -col[0:3, 256:384]


def from_behind(block, axis, distance):
    count = lax.axis_size(axis)
    route = [((i - distance) % count, i) for i in range(count)]
    return lax.ppermute(block, axis, route)


def eye(n):
    r = lax.broadcasted_iota(jnp.int32, (n, n), 0)
    return (r == lax.broadcasted_iota(jnp.int32, (n, n), 1)).astype(f32)


def turned(x):
    return lax.dot_general(
        eye(x.shape[1]), x, (((1,), (1,)), ((), ())), precision=lax.Precision.HIGHEST,
        preferred_element_type=f32,
    )


def left3(x):
    hi = x.astype(bf16).astype(f32)
    return jnp.concatenate([hi, hi, x - hi], axis=-1).astype(bf16)


def stacked(x):
    hi = x.astype(bf16).astype(f32)
    return jnp.concatenate([hi, x - hi], axis=0).astype(bf16)


def prepare_kernel(
    emb, rin, rmid, rout1, rout2, mix, mo1, mo2, c1, c2, lin, rh, ro,
    f1, s1, t1, f2, s2, t2, tt1, st1, ft1, tt2, st2, ft2, mf1, mb1, mf2, mb2, of1, ob1, of2, ob2,
    k1, k2, embo, lino, rho, rhto, roo, pad,
):
    for t, (f, s, o, tt, st, ft, out, mf, mb) in enumerate(
        ((f1, s1, t1, tt1, st1, ft1, rout1, mf1, mb1), (f2, s2, t2, tt2, st2, ft2, rout2, mf2, mb2))
    ):
        x = rin[t]
        hi = x.astype(bf16).astype(f32)
        top = turned(jnp.concatenate([hi, hi], axis=0))
        low = turned(jnp.concatenate([x - hi, jnp.zeros_like(x)], axis=0))
        f[...] = jnp.concatenate([top, low], axis=0).astype(bf16)
        s[...] = left3(turned(rmid[t]))
        for p in range(o.shape[0] // CH):
            o[p * CH : (p + 1) * CH, :] = left3(turned(out[:, lanes(p)]))
        tt[...] = stacked(out[...])
        st[...] = left3(rmid[t])
        ft[...] = left3(jnp.concatenate([x, jnp.zeros_like(x)], axis=0))
        for l in range(3):
            mf[l] = left3(turned(mix[t, l]))
            mb[l] = left3(mix[t, l])
    for l in range(3):
        of1[l] = left3(turned(mo1[l]))
        ob1[l] = left3(mo1[l])
    of2[...] = left3(turned(mo2[...]))
    ob2[...] = left3(mo2[...])
    k1[...] = turned(c1[...])
    k2[...] = turned(c2[...])
    pad[...] = jnp.zeros_like(pad)
    pad[0 : emb.shape[0], :] = emb[...]
    embo[...] = stacked(turned(pad[...]))
    lino[...] = turned(lin[...])
    rho[...] = left3(rh[...])
    rhto[...] = left3(turned(rh[...]))
    roo[...] = turned(ro[...])


def prepare(embedding, radial_in, radial_mid, outs, mix, mix_out_one, mix_out_two, product_one, product_two, read_lin, read_hidden, read_out):
    def half(*dims):
        return shape(*dims, kind=bf16)

    paths = [o.shape[1] for o in outs]
    small = lambda n: [half(128, 16), half(HID, 192), half(n, 192)]
    back = lambda n: [half(128, n), half(HID, 192), half(16, 192)]
    square = half(CH, 384)
    three = half(3, CH, 384)
    names = ("r1", "r2", "b1", "b2")
    shapes = small(paths[0]) + small(paths[1]) + back(paths[0]) + back(paths[1])
    shapes += [three] * 6 + [square] * 2
    shapes += [shape(CH, 5), shape(CH, 3), half(256, CH), shape(CH, 1), half(CH, 48), half(16, 384), shape(16, 1)]
    got = call(prepare_kernel, tuple(shapes), scratch=[pltpu.VMEM((CH, CH), f32)], flops=4000000000)(
        embedding, radial_in, radial_mid, *outs, mix, mix_out_one, mix_out_two, product_one,
        product_two, read_lin[None], read_hidden, read_out[None],
    )
    w = {n: tuple(got[3 * i : 3 * i + 3]) for i, n in enumerate(names)}
    rest = ("mf1", "mb1", "mf2", "mb2", "of1", "ob1", "of2", "ob2", "coef1", "coef2", "emb", "lin", "rh", "rht", "ro")
    w.update(zip(rest, got[12:]))
    return w


def on_device(
    positions, species, dest_key, send_list, send_count, border, neighbours, embedding, radial_in,
    radial_mid, radial_out_one, radial_out_two, mix, mix_out_one, mix_out_two, product_one,
    product_two, read_lin, read_hidden, read_out,
):
    pos = positions[0, 0]
    spec = species[0]
    key = dest_key[0]
    rows = border[0]
    nbr = neighbours[0, 0].T
    packet = call(
        packet_kernel,
        shape(8, 256),
        scratch=[pltpu.VMEM((8, 256), f32)],
        in_specs=[VMEM, VMEM, VMEM, VMEM, SMEM],
    )(pos, spec, send_list.reshape(1, LANES), rows, send_count.reshape(4))
    xp = from_behind(packet, "gx", 1)
    xn = from_behind(packet, "gx", -1)
    wide = jnp.concatenate([packet, xp[:, LANES:], xn[:, LANES:]], axis=1)
    yp = from_behind(wide, "gy", 1)
    yn = from_behind(wide, "gy", -1)
    w = prepare(embedding, radial_in, radial_mid, (radial_out_one, radial_out_two), mix, mix_out_one,
                mix_out_two, product_one, product_two, read_lin, read_hidden, read_out)
    geo, bgeo, vcol, kinds, occ = call(
        edges_kernel,
        (
            shape(LOCAL, 64, LANES),
            shape(64, LANES),
            shape(LOCAL, 16, LANES, kind=jnp.int32),
            shape(1, COLS),
            shape(1, LOCAL * LANES),
        ),
        scratch=[pltpu.VMEM((8, COLS), f32)],
    )(pos, spec, key, xp, xn, yp, yn, nbr, rows)
    gxp = from_behind(bgeo, "gx", 1)
    gxn = from_behind(bgeo, "gx", -1)
    tl, kl = layer_one(geo, kinds[:, :384], NL, w)
    three = jnp.stack([gxp, bgeo, gxn])
    gyp = from_behind(three, "gy", 1)
    gyn = from_behind(three, "gy", -1)
    geo_x = jnp.stack([gxp, gxn])
    tx, kx = layer_one(geo_x, kinds[:, 384:640], NX, w)
    geo_y = jnp.concatenate([gyp, gyn], axis=0)
    ty, ky = layer_one(geo_y, kinds[:, 640:], NY, w)
    energy, dl, dx, dy, g2 = layer_two(tl, tx, ty, geo, vcol, occ, w)
    dgy = layer_one_back(geo_y, dy, ky, 1, w)
    ry1 = from_behind(dgy[0:3], "gy", -1)
    ry2 = from_behind(dgy[3:6], "gy", 1)
    dgx = layer_one_back(geo_x, dx, kx, 1, w)
    rx1 = from_behind(dgx[0] + ry1[0] + ry2[0], "gx", -1)
    rx2 = from_behind(dgx[1] + ry1[2] + ry2[2], "gx", 1)
    g1 = layer_one_back(geo, dl, kl, 1, w)
    col = call(
        columns_kernel,
        shape(8, COLS),
        scratch=[
            pltpu.VMEM((LOCAL, 64, LANES), f32),
            pltpu.VMEM((11 * 16, EDGES), bf16),
            pltpu.VMEM((LANES, EDGES), bf16),
        ],
    )(g2, g1, ry1[1], ry2[1], rx1, rx2, vcol, rows)
    r1 = from_behind(col[:, 640:1024], "gy", -1)
    r2 = from_behind(col[:, 1024:1408], "gy", 1)
    sx1 = from_behind(col[:, 384:512] + r1[:, 0:128] + r2[:, 0:128], "gx", -1)
    sx2 = from_behind(col[:, 512:640] + r1[:, 256:384] + r2[:, 256:384], "gx", 1)
    forces = call(forces_kernel, shape(3, LOCAL * LANES))(col, r1, r2, sx1, sx2, rows)
    return energy[None], forces[None, None]


def solution(mesh):
    along = P("gx", "gy")
    in_specs = (along,) * 7 + (P(),) * 13
    return jax.shard_map(
        on_device, mesh=mesh, in_specs=in_specs, out_specs=(along, along), check_vma=False
    )
```

```python
import functools
import math

import jax
import jax.numpy as jnp
from jax import lax
from jax.experimental import pallas as pl
from jax.experimental.pallas import tpu as pltpu
from jax.sharding import PartitionSpec as P

f32 = jnp.float32
bf16 = jnp.bfloat16
CH = 128
HID = 64
SLOTS = 12
LANES = 128
EDGES = SLOTS * LANES
LOCAL = 3
COLS = 11 * LANES
NL, NX, NY = 1, 2, 2
RADIUS = 5.0
SCALE = math.sqrt(2.0 / RADIUS)
R3 = math.sqrt(3.0)
R5 = math.sqrt(5.0)
R15 = math.sqrt(15.0)
VMEM = pl.BlockSpec(memory_space=pltpu.VMEM)
SMEM = pl.BlockSpec(memory_space=pltpu.SMEM)
LIMIT = 60 * 1024 * 1024


def call(kernel, out_shape, scratch=(), flops=1000000, in_specs=None, **kw):
    return pl.pallas_call(
        kernel,
        out_shape=out_shape,
        scratch_shapes=list(scratch),
        compiler_params=pltpu.CompilerParams(vmem_limit_bytes=LIMIT),
        cost_estimate=pl.CostEstimate(flops=flops, bytes_accessed=1000000, transcendentals=0),
        **({"in_specs": in_specs} if in_specs is not None else {}),
        **kw,
    )


def shape(*dims, kind=f32):
    return jax.ShapeDtypeStruct(dims, kind)


def lanes(i, n=1):
    return slice(i * LANES, (i + n) * LANES)


def hi_lo(x):
    hi = x.astype(bf16)
    return hi, (x - hi.astype(f32)).astype(bf16)


def split3(x):
    hi, lo = hi_lo(x)
    return jnp.concatenate([hi, lo, hi], axis=0)


def mm(a, b):
    return jnp.dot(a, b, preferred_element_type=f32)


def mm_nt(a, b):
    return lax.dot_general(a, b, (((1,), (1,)), ((), ())), preferred_element_type=f32)


def silu_parts(x):
    s = 0.5 * jnp.tanh(0.5 * x) + 0.5
    h = x * s
    return h, s + h * (1.0 - s)


def take_lanes(chunk, index):
    return jnp.take_along_axis(chunk, index, axis=1, mode="promise_in_bounds")


def gather_columns(ref, rows, index, chunks):
    low = index & 127
    block = index >> 7
    out = take_lanes(ref[rows, lanes(0)], low)
    for c in range(1, chunks):
        out = jnp.where(block == c, take_lanes(ref[rows, lanes(c)], low), out)
    return out


def packet_kernel(pos, spec, listed, border, count, out, tbl):
    tbl[...] = jnp.zeros_like(tbl)
    tbl[0:3, :] = pos[...]
    tbl[3:4, :] = spec[...].astype(f32)
    row = lax.broadcasted_iota(jnp.int32, (8, LANES), 0)
    lane = lax.broadcasted_iota(jnp.int32, (8, LANES), 1)
    way = lane >> 5
    index = jnp.broadcast_to(listed[...], (8, LANES))
    got = gather_columns(tbl, slice(0, 8), index, 2)
    amount = jnp.where(way == 0, count[0], jnp.where(way == 1, count[1], jnp.where(way == 2, count[2], count[3])))
    step = jnp.where((way & 1) == 0, -1.0, 1.0).astype(f32)
    got = got + jnp.where(row == (way >> 1), step, 0.0)
    got = jnp.where((row == 3) & ((lane & 31) >= amount), -1.0, got)
    out[:, lanes(0)] = got
    out[:, lanes(1)] = gather_columns(tbl, slice(0, 8), jnp.broadcast_to(border[...], (8, LANES)), 2)


PLACE = {1: 3, 7: 4, 0: 5, 3: 6, 6: 7, 2: 8, 5: 9, 8: 10}


def edges_kernel(pos, spec, key, xp, xn, yp, yn, nbr, border, geo, bgeo, vcol, kinds_l, kinds_x, kinds_y, occ, tbl):
    tbl[...] = jnp.zeros_like(tbl)
    tbl[0:3, 0:256] = pos[...]
    tbl[3:4, 0:256] = spec[...].astype(f32)
    tbl[4:5, 0:256] = (key[...] == 0).astype(f32)
    row = lax.broadcasted_iota(jnp.int32, (8, LANES), 0)
    way = lax.broadcasted_iota(jnp.int32, (8, LANES), 1) >> 5
    came = jnp.where(
        way == 0,
        xp[:, lanes(0)],
        jnp.where(way == 1, xn[:, lanes(0)], jnp.where(way == 2, yp[:, lanes(0)], yn[:, lanes(0)])),
    )
    tbl[:, lanes(2)] = came
    tbl[4:5, lanes(2)] = (came[3:4] >= 0).astype(f32)

    def ghost(place, block, dx, dy):
        moved = block + jnp.where(row == 0, dx, jnp.where(row == 1, dy, jnp.where(row == 4, 1.0, 0.0)))
        tbl[:, lanes(place)] = moved

    ghost(3, xp[:, lanes(1)], -1.0, 0.0)
    ghost(4, xn[:, lanes(1)], 1.0, 0.0)
    for base, got, dy in ((5, yp, -1.0), (8, yn, 1.0)):
        ghost(base, got[:, lanes(2)], -1.0, dy)
        ghost(base + 1, got[:, lanes(1)], 0.0, dy)
        ghost(base + 2, got[:, lanes(3)], 1.0, dy)
    kinds_l[...] = jnp.maximum(tbl[3:4, 0:384], 0.0)
    kinds_x[...] = jnp.maximum(tbl[3:4, 384:640], 0.0)
    kinds_y[...] = jnp.maximum(tbl[3:4, 640:1408], 0.0)
    occ[...] = tbl[4:5, 0 : LOCAL * LANES]
    geo[...] = jnp.zeros_like(geo)
    vcol[...] = jnp.full_like(vcol, -1)
    for b in range(LOCAL):
        own = tbl[:, lanes(b)]
        for s in range(SLOTS):
            n = nbr[s : s + 1, lanes(b)]
            old = n >> 7
            block = jnp.minimum(old, 2)
            for was, now in PLACE.items():
                block = jnp.where(old == was + 3, now, block)
            col = jnp.maximum(block, 0) * 128 + (n & 127)
            got = gather_columns(tbl, slice(0, 8), jnp.broadcast_to(col, (8, LANES)), 11)
            valid = (n >= 0) & (got[4:5] > 0.5) & (own[4:5] > 0.5)
            off = got - own
            val = jnp.where(row < 3, off, jnp.where(jnp.broadcast_to(valid, (8, LANES)), got, -1.0))
            geo[b, pl.ds(s, 4, stride=16), :] = val[0:4]
            vcol[b, s : s + 1, :] = jnp.where(valid, col, -1)
    index = jnp.broadcast_to(border[...], (8, LANES))
    low = index & 127
    for t in range(8):
        rows = slice(t * 8, t * 8 + 8)
        bgeo[rows, :] = jnp.where(
            (index >> 7) == 0, take_lanes(geo[0, rows, :], low), take_lanes(geo[1, rows, :], low)
        )


def geometry(ox, oy, oz):
    d = jnp.sqrt(ox * ox + oy * oy + oz * oz + 1.0)
    rd = 1.0 / d
    u = (ox * rd, oy * rd, oz * rd)
    t = d * (1.0 / RADIUS)
    t2 = t * t
    t5 = t2 * t2 * t
    t6 = t5 * t
    env = 1.0 - 28.0 * t6 + 48.0 * t6 * t - 21.0 * t6 * t2
    theta = (math.pi / RADIUS) * d
    s1, c1 = jnp.sin(theta), jnp.cos(theta)
    sines, cosines = [s1], [c1]
    before_s, before_c = jnp.zeros_like(s1), jnp.ones_like(c1)
    for _ in range(7):
        ns = 2.0 * c1 * sines[-1] - before_s
        nc = 2.0 * c1 * cosines[-1] - before_c
        before_s, before_c = sines[-1], cosines[-1]
        sines.append(ns)
        cosines.append(nc)
    slope = (-168.0 * t5 + 336.0 * t6 - 168.0 * t6 * t) * (1.0 / RADIUS)
    return u, d, rd, env, slope, sines, cosines


def harmonics(u):
    x, y, z = u
    return [
        R3 * x,
        R3 * y,
        R3 * z,
        R15 * x * y,
        R15 * y * z,
        0.5 * R5 * (2.0 * z * z - x * x - y * y),
        R15 * x * z,
        0.5 * R15 * (x * x - y * y),
    ]


def place_geometry(geo, yref, basrow, bas):
    u, d, rd, env, slope, sines, cosines = geo
    for k, h in enumerate(harmonics(u)):
        yref[k * 16 : k * 16 + 16, :] = h
    factor = SCALE * env * rd
    for m in range(8):
        basrow[m * 16 : m * 16 + 16, :] = sines[m] * factor
    for s in range(SLOTS):
        got = basrow[pl.ds(s, 8, stride=16), :]
        bas[0:8, lanes(s)] = got
        bas[8:16, lanes(s)] = got - got.astype(bf16).astype(f32)


def geometry_back(geo, dyref, dbas):
    (x, y, z), d, rd, env, slope, sines, cosines = geo
    g = [dyref[k * 16 : k * 16 + 16, :] for k in range(8)]
    dx = R3 * g[0] + R15 * (y * g[3] + z * g[6] + x * g[7]) - R5 * x * g[5]
    dy = R3 * g[1] + R15 * (x * g[3] + z * g[4] - y * g[7]) - R5 * y * g[5]
    dz = R3 * g[2] + R15 * (y * g[4] + x * g[6]) + 2.0 * R5 * z * g[5]
    along = jnp.zeros_like(x)
    turned = jnp.zeros_like(x)
    for m in range(8):
        db = dbas[m * 16 : m * 16 + 16, :]
        along = along + db * sines[m]
        turned = turned + ((m + 1) * math.pi / RADIUS) * db * cosines[m]
    dd = SCALE * rd * (turned * env + along * (slope - env * rd))
    dd = dd - (dx * x + dy * y + dz * z) * rd
    return dx * rd + x * dd, dy * rd + y * dd, dz * rd + z * dd


def radial_forward(bas, first, second, third, wref, e1=None, e2=None):
    pre = mm(first[...], bas[...].astype(bf16))
    h, e = silu_parts(pre[:HID] + pre[HID:])
    if e1 is not None:
        e1[...] = e
    h, e = silu_parts(mm(second[...], split3(h)))
    if e2 is not None:
        e2[...] = e
    h = split3(h)
    for p in range(third.shape[0] // CH):
        wref[p * CH : (p + 1) * CH, :] = mm(third[p * CH : (p + 1) * CH, :], h)


def radial_back(dwref, third_t, second_t, first_t, e1, e2, dbrow, dbas):
    both = mm(third_t[...], dwref[...])
    dp = (both[:HID] + both[HID:]) * e2[...]
    dp = mm(second_t[...], split3(dp)) * e1[...]
    dbrow[...] = mm(first_t[...], split3(dp))
    dbas[...] = jnp.zeros_like(dbas)
    for s in range(SLOTS):
        dbas[pl.ds(s, 8, stride=16), :] = dbrow[0:8, lanes(s)]


ORDERS = ((0, 1), (1, 3), (4, 5))


def mixed(matrices, values, out):
    for l, (start, n) in enumerate(ORDERS):
        out[:, lanes(start, n)] = mm(matrices[l], split3(values[:, lanes(start, n)]))


def sum_of(terms):
    total = terms[0]
    for t in terms[1:]:
        total = total + t
    return total


def first_features(geo, emb, fref):
    iota = lax.broadcasted_iota(jnp.int32, (CH, LANES), 0)
    for s in range(SLOTS):
        kind = geo[48 + s : 49 + s, :].astype(jnp.int32)
        hot = (iota == kind).astype(f32).astype(bf16)
        both = mm(emb[...], hot)
        fref[:, lanes(s)] = both[:CH] + both[CH:]


def ctiles():
    return [slice(c * 16, c * 16 + 16) for c in range(CH // 16)]


def layer_one_kernel(many, geos, kinds, first, second, third, emb, mf, mo, coef, out, keeps, *scratch):
    sets = [scratch[6 * q : 6 * q + 6] for q in range(many)]
    for q, (yref, basrow, bas, wref, fref, aref) in enumerate(sets):
        geo = geos.at[q]
        place_geometry(geometry(geo[0:16, :], geo[16:32, :], geo[32:48, :]), yref, basrow, bas)
    for q, (yref, basrow, bas, wref, fref, aref) in enumerate(sets):
        radial_forward(bas, first, second, third, wref)
        first_features(geos.at[q], emb, fref)

    def messages(c, _):
        r0 = pl.ds(pl.multiple_of(c * 16, 16), 16)
        r1 = pl.ds(pl.multiple_of(c * 16 + CH, 16), 16)
        r2 = pl.ds(pl.multiple_of(c * 16 + 2 * CH, 16), 16)
        for yref, basrow, bas, wref, fref, aref in sets:
            acc = [None] * 9

            def add(k, v):
                acc[k] = v if acc[k] is None else acc[k] + v

            for s in range(SLOTS):
                f = fref[r0, lanes(s)]
                add(0, wref[r0, lanes(s)] * f)
                w1 = wref[r1, lanes(s)] * f
                w2 = wref[r2, lanes(s)] * f
                for k in range(8):
                    add(k + 1, (w1 if k < 3 else w2) * yref[k * 16 + s : k * 16 + s + 1, :])
            for k in range(9):
                aref[r0, lanes(k)] = acc[k] * (1.0 / SLOTS)
        return 0

    lax.fori_loop(0, CH // 16, messages, 0, unroll=True)
    for q in range(many):
        mixed(mf, sets[q][5], keeps.at[q])
    for q in range(many):
        keep, aref = keeps.at[q], sets[q][5]
        for r in ctiles():
            p = [keep[r, lanes(k)] for k in range(9)]
            c = [coef[r, k : k + 1] for k in range(5)]
            aref[r, lanes(0)] = (
                p[0]
                + c[0] * p[0] * p[0]
                + c[1] * sum_of([p[k] * p[k] for k in range(1, 4)])
                + c[2] * sum_of([p[k] * p[k] for k in range(4, 9)])
            )
            up, ut = 1.0 + c[3] * p[0], 1.0 + c[4] * p[0]
            for k in range(1, 9):
                aref[r, lanes(k)] = p[k] * (up if k < 4 else ut)
    iota = lax.broadcasted_iota(jnp.int32, (CH, LANES), 0)
    for q in range(many):
        aref = sets[q][5]
        hot = (iota == kinds[:, lanes(q)].astype(jnp.int32)).astype(f32).astype(bf16)
        both = mm(emb[...], hot)
        out[0:CH, lanes(q)] = (mm(mo[0], split3(aref[:, lanes(0)])) + (both[:CH] + both[CH:])).astype(bf16)
        for l, (start, n) in enumerate(ORDERS[1:], 1):
            got = mm(mo[l], split3(aref[:, lanes(start, n)]))
            for k in range(n):
                out[(start + k) * CH : (start + k + 1) * CH, lanes(q)] = got[:, lanes(k)].astype(bf16)


def whole(a):
    rank = len(a.shape)
    return pl.BlockSpec(a.shape, lambda i: (0,) * rank)


def layer_one(geo, kinds, many, weights):
    n = geo.shape[0]
    first, second, third = weights["r1"]
    consts = (first, second, third, weights["emb"], weights["mf1"], weights["of1"], weights["coef1"])
    return call(
        functools.partial(layer_one_kernel, many),
        (shape(9 * CH, n * LANES, kind=bf16), shape(n, CH, 9 * LANES)),
        grid=(n // many,),
        in_specs=[
            pl.BlockSpec((many, 64, LANES), lambda i: (i, 0, 0)),
            pl.BlockSpec((1, many * LANES), lambda i: (0, i)),
        ]
        + [whole(a) for a in consts],
        out_specs=(
            pl.BlockSpec((9 * CH, many * LANES), lambda i: (0, i)),
            pl.BlockSpec((many, CH, 9 * LANES), lambda i: (i, 0, 0)),
        ),
        scratch=[
            pltpu.VMEM((128, LANES), f32),
            pltpu.VMEM((128, LANES), f32),
            pltpu.VMEM((16, EDGES), f32),
            pltpu.VMEM((3 * CH, EDGES), f32),
            pltpu.VMEM((CH, EDGES), f32),
            pltpu.VMEM((CH, 9 * LANES), f32),
        ]
        * many,
        flops=n * 900000000,
    )(geo, kinds, *consts)


def layer_one_back_kernel(
    many, geos, grad, keeps, first, second, third, third_t, second_t, first_t, emb, mb, mo, coef, out, *scratch
):
    sets = [scratch[13 * q : 13 * q + 13] for q in range(many)]
    geoms = []
    for q in range(many):
        geo, (yref, basrow, bas) = geos.at[q], sets[q][:3]
        geoms.append(geometry(geo[0:16, :], geo[16:32, :], geo[32:48, :]))
        place_geometry(geoms[q], yref, basrow, bas)
    for q in range(many):
        yref, basrow, bas, wref, fref, aref, dref, e1, e2, dwref, dyref, dbrow, dbas = sets[q]
        radial_forward(bas, first, second, third, wref, e1, e2)
        first_features(geos.at[q], emb, fref)
    for q in range(many):
        aref, dref = sets[q][5:7]
        for k in range(9):
            aref[:, lanes(k)] = grad[k * CH : (k + 1) * CH, lanes(q)]
        mixed(mo, aref, dref)
    for q in range(many):
        aref, dref = sets[q][5:7]
        keep = keeps.at[q]
        for r in ctiles():
            p = [keep[r, lanes(k)] for k in range(9)]
            g = [dref[r, lanes(k)] for k in range(9)]
            c = [coef[r, k : k + 1] for k in range(5)]
            aref[r, lanes(0)] = (1.0 / SLOTS) * (
                g[0] * (1.0 + 2.0 * c[0] * p[0])
                + c[3] * sum_of([p[k] * g[k] for k in range(1, 4)])
                + c[4] * sum_of([p[k] * g[k] for k in range(4, 9)])
            )
            g = [v * (1.0 / SLOTS) for v in g]
            up, ut = 1.0 + c[3] * p[0], 1.0 + c[4] * p[0]
            vp, vt = 2.0 * c[1] * g[0], 2.0 * c[2] * g[0]
            for k in range(1, 9):
                aref[r, lanes(k)] = g[k] * (up if k < 4 else ut) + p[k] * (vp if k < 4 else vt)
    for q in range(many):
        mixed(mb, *sets[q][5:7])
        sets[q][10][...] = jnp.zeros_like(sets[q][10])

    def slot(s, _):
        here = pl.ds(pl.multiple_of(s * LANES, LANES), LANES)
        for yref, basrow, bas, wref, fref, aref, dref, e1, e2, dwref, dyref, dbrow, dbas in sets:
            y = [yref[pl.ds(k * 16 + s, 1), :] for k in range(8)]
            dy = [None] * 8
            for c in range(CH // 16):
                r0, r1, r2 = (slice(q * CH + c * 16, q * CH + c * 16 + 16) for q in range(3))
                f = fref[r0, here]
                w1 = wref[r1, here] * f
                w2 = wref[r2, here] * f
                d = [dref[r0, lanes(k)] for k in range(9)]
                dwref[r0, here] = (d[0] * f).astype(bf16)
                dwref[r1, here] = (f * sum_of([d[k + 1] * y[k] for k in range(3)])).astype(bf16)
                dwref[r2, here] = (f * sum_of([d[k + 1] * y[k] for k in range(3, 8)])).astype(bf16)
                for k in range(8):
                    v = (w1 if k < 3 else w2) * d[k + 1]
                    v = v[0:8] + v[8:16]
                    dy[k] = v if dy[k] is None else dy[k] + v
            for k in range(8):
                dyref[pl.ds(k * 16 + s, 1), :] = jnp.sum(dy[k], axis=0, keepdims=True)
        return 0

    lax.fori_loop(0, SLOTS, slot, 0, unroll=True)
    for yref, basrow, bas, wref, fref, aref, dref, e1, e2, dwref, dyref, dbrow, dbas in sets:
        radial_back(dwref, third_t, second_t, first_t, e1, e2, dbrow, dbas)
    for q in range(many):
        dx, dy, dz = geometry_back(geoms[q], sets[q][10], sets[q][12])
        out[q, 0:16, :] = dx
        out[q, 16:32, :] = dy
        out[q, 32:48, :] = dz


def layer_one_back(geo, grad, keep, many, weights):
    n = geo.shape[0]
    first, second, third = weights["r1"]
    consts = (first, second, third) + weights["b1"] + (
        weights["emb"], weights["mb1"], weights["ob1"], weights["coef1"])
    return call(
        functools.partial(layer_one_back_kernel, many),
        shape(n, 48, LANES),
        grid=(n // many,),
        in_specs=[
            pl.BlockSpec((many, 64, LANES), lambda i: (i, 0, 0)),
            pl.BlockSpec((9 * CH, many * LANES), lambda i: (0, i)),
            pl.BlockSpec((many, CH, 9 * LANES), lambda i: (i, 0, 0)),
        ]
        + [whole(a) for a in consts],
        out_specs=pl.BlockSpec((many, 48, LANES), lambda i: (i, 0, 0)),
        scratch=[
            pltpu.VMEM((128, LANES), f32),
            pltpu.VMEM((128, LANES), f32),
            pltpu.VMEM((16, EDGES), f32),
            pltpu.VMEM((3 * CH, EDGES), f32),
            pltpu.VMEM((CH, EDGES), f32),
            pltpu.VMEM((CH, 9 * LANES), f32),
            pltpu.VMEM((CH, 9 * LANES), f32),
            pltpu.VMEM((HID, EDGES), f32),
            pltpu.VMEM((HID, EDGES), f32),
            pltpu.VMEM((3 * CH, EDGES), bf16),
            pltpu.VMEM((128, LANES), f32),
            pltpu.VMEM((16, EDGES), f32),
            pltpu.VMEM((128, LANES), f32),
        ]
        * many,
        flops=n * 2000000000,
    )(geo, grad, keep, *consts)


def build_hot(vcol, b, hot, s):
    iota = lax.broadcasted_iota(jnp.int32, (COLS, LANES), 0)
    v = vcol[b, s : s + 1, :]
    hot[:, lanes(b * SLOTS + s)] = (iota == v).astype(f32).astype(bf16)


def layer_two_kernel(
    tl, tx, ty, geos, vcol, occ, first, second, third, third_t, second_t, first_t, mf, mb, of, ob,
    coef, lin, rh, rht, ro, energy, dl, dx_, dy_, dgeo,
    tab, yref, basrow, bas, wref, aref, dref, e1, e2, dwref, dyref, dbrow, dbas,
    hot, gat0, gat1, dgat,
):
    gats = (gat0, gat1, gat0)
    tab[:, 0:384] = tl[...]
    tab[:, 384:640] = tx[...]
    tab[:, 640:1408] = ty[...]
    dyref[...] = jnp.zeros_like(dyref)

    def gather(b, j):
        here = pl.ds(pl.multiple_of(j * 256, 256), 256)
        there = pl.ds(pl.multiple_of(b * EDGES + j * 256, 256), 256)
        gats[b][:, here] = mm(tab[...], hot[:, there]).astype(bf16)

    def messages(gat, c):
        acc = [None] * 9

        def add(k, v):
            acc[k] = v if acc[k] is None else acc[k] + v

        r = [pl.ds(pl.multiple_of(c * 16 + q * CH, 16), 16) for q in range(9)]
        for s in range(SLOTS):
            y = [yref[k * 16 + s : k * 16 + s + 1, :] for k in range(8)]
            x = [gat[r[q], lanes(s)].astype(f32) for q in range(9)]
            w = [wref[r[q], lanes(s)] for q in range(7)]
            a1 = sum_of([y[k] * x[k + 1] for k in range(3)])
            a2 = sum_of([y[k] * x[k + 1] for k in range(3, 8)])
            add(0, w[0] * x[0] + w[1] * a1 + w[2] * a2)
            t1, t2 = w[3] * x[0], w[5] * x[0]
            for k in range(8):
                add(k + 1, (t1 if k < 3 else t2) * y[k] + (w[4] if k < 3 else w[6]) * x[k + 1])
        for k in range(9):
            aref[r[0], lanes(k)] = acc[k] * (1.0 / SLOTS)

    def middle(b):
        mixed(mf, aref, dref)
        for r in ctiles():
            p = [dref[r, lanes(k)] for k in range(9)]
            c = [coef[r, k : k + 1] for k in range(3)]
            aref[r, lanes(0)] = (
                p[0]
                + c[0] * p[0] * p[0]
                + c[1] * sum_of([p[k] * p[k] for k in range(1, 4)])
                + c[2] * sum_of([p[k] * p[k] for k in range(4, 9)])
            )
        base = tab[0:CH, lanes(b)].astype(f32)
        scal = mm(of[...], split3(aref[:, lanes(0)])) + base
        h, e = silu_parts(mm(rht[...], split3(scal)))
        mask = occ[:, lanes(b)]
        tot = jnp.sum(ro[...] * h, axis=0, keepdims=True) + jnp.sum(lin[...] * base, axis=0, keepdims=True)
        energy[:, lanes(b)] = tot * mask
        ds = mm(rh[...], split3(ro[...] * e * mask))
        dl[0:CH, lanes(b)] = ds + lin[...] * mask
        aref[:, lanes(1)] = mm(ob[...], split3(ds * (1.0 / SLOTS)))
        for r in ctiles():
            db = aref[r, lanes(1)]
            c = [coef[r, k : k + 1] for k in range(3)]
            aref[r, lanes(0)] = db * (1.0 + 2.0 * c[0] * dref[r, lanes(0)])
            dp, dt = 2.0 * c[1] * db, 2.0 * c[2] * db
            for k in range(1, 9):
                aref[r, lanes(k)] = (dp if k < 4 else dt) * dref[r, lanes(k)]
        mixed(mb, aref, dref)

    def slot(gat, b, s):
        here = pl.ds(pl.multiple_of(s * LANES, LANES), LANES)
        there = pl.ds(pl.multiple_of(b * EDGES + s * LANES, LANES), LANES)
        y = [yref[pl.ds(k * 16 + s, 1), :] for k in range(8)]
        dy = [None] * 8
        for cc in range(CH // 16):
            r = [slice(q * CH + cc * 16, q * CH + cc * 16 + 16) for q in range(9)]
            x = [gat[r[q], here].astype(f32) for q in range(9)]
            w = [wref[r[q], here] for q in range(7)]
            d = [dref[r[0], lanes(k)] for k in range(9)]
            t1 = sum_of([y[k] * d[k + 1] for k in range(3)])
            t2 = sum_of([y[k] * d[k + 1] for k in range(3, 8)])
            a1 = sum_of([y[k] * x[k + 1] for k in range(3)])
            a2 = sum_of([y[k] * x[k + 1] for k in range(3, 8)])
            b1 = sum_of([d[k + 1] * x[k + 1] for k in range(3)])
            b2 = sum_of([d[k + 1] * x[k + 1] for k in range(3, 8)])
            dgat[r[0], there] = (w[0] * d[0] + w[3] * t1 + w[5] * t2).astype(bf16)
            m1, m2 = w[1] * d[0], w[2] * d[0]
            n1, n2 = w[3] * x[0], w[5] * x[0]
            for k in range(8):
                m, n, q = (m1, n1, w[4]) if k < 3 else (m2, n2, w[6])
                dgat[r[k + 1], there] = (m * y[k] + q * d[k + 1]).astype(bf16)
                v = m * x[k + 1] + n * d[k + 1]
                v = v[0:8] + v[8:16]
                dy[k] = v if dy[k] is None else dy[k] + v
            for q, v in enumerate((d[0] * x[0], d[0] * a1, d[0] * a2, x[0] * t1, b1, x[0] * t2, b2)):
                dwref[r[q], here] = v.astype(bf16)
        for k in range(8):
            dyref[pl.ds(k * 16 + s, 1), :] = jnp.sum(dy[k], axis=0, keepdims=True)

    def loop(n, *parts):
        def body(j, _):
            for part in parts:
                part(j)
            return 0

        lax.fori_loop(0, n, body, 0)

    for s in range(SLOTS):
        build_hot(vcol, 0, hot, s)
    geoms = [geometry(*(geos[b, k * 16 : k * 16 + 16, :] for k in range(3))) for b in range(LOCAL)]
    for b in range(LOCAL):
        gat = gats[b]
        place_geometry(geoms[b], yref, basrow, bas)
        radial_forward(bas, first, second, third, wref, e1, e2)
        if b == 0:
            for j in range(6):
                gather(0, j)
                for q in (2 * j, 2 * j + 1):
                    build_hot(vcol, 1, hot, q)
                    build_hot(vcol, 2, hot, q)
        loop(CH // 16, lambda c: messages(gat, c))
        middle(b)

        def slots(j):
            slot(gat, b, 2 * j)
            slot(gat, b, 2 * j + 1)

        if b + 1 < LOCAL:
            loop(6, slots, lambda j: gather(b + 1, j))
        else:
            loop(6, slots)
        radial_back(dwref, third_t, second_t, first_t, e1, e2, dbrow, dbas)
        gx, gy, gz = geometry_back(geoms[b], dyref, dbas)
        dgeo[b, 0:16, :] = gx
        dgeo[b, 16:32, :] = gy
        dgeo[b, 32:48, :] = gz
    def ghosts(j):
        here = pl.ds(pl.multiple_of(j * 256, 256), 256)
        dy_[:, here] = mm_nt(dgat[...], hot[pl.ds(pl.multiple_of(640 + j * 256, 128), 256), :])

    loop(3, ghosts)
    for out, place, start, size in PIECES:
        out = (dl, dx_, dy_)[out]
        got = mm_nt(dgat[...], hot[start : start + size, :])
        here = slice(place, place + size)
        if out is dl:
            out[0:CH, here] = out[0:CH, here] + got[0:CH]
            out[CH:, here] = got[CH:]
        else:
            out[:, here] = got


PIECES = ((0, 0, 0, 256), (0, 256, 256, 128), (1, 0, 384, 256))


def layer_two(tl, tx, ty, geo, vcol, occ, w):
    first, second, third = w["r2"]
    return call(
        layer_two_kernel,
        (shape(1, LOCAL * LANES), shape(9 * CH, 384), shape(9 * CH, 256), shape(9 * CH, 768), shape(LOCAL, 48, LANES)),
        scratch=[
            pltpu.VMEM((9 * CH, COLS), bf16),
            pltpu.VMEM((128, LANES), f32),
            pltpu.VMEM((128, LANES), f32),
            pltpu.VMEM((16, EDGES), f32),
            pltpu.VMEM((7 * CH, EDGES), f32),
            pltpu.VMEM((CH, 9 * LANES), f32),
            pltpu.VMEM((CH, 9 * LANES), f32),
            pltpu.VMEM((HID, EDGES), f32),
            pltpu.VMEM((HID, EDGES), f32),
            pltpu.VMEM((7 * CH, EDGES), bf16),
            pltpu.VMEM((128, LANES), f32),
            pltpu.VMEM((16, EDGES), f32),
            pltpu.VMEM((128, LANES), f32),
        ]
        + [pltpu.VMEM((COLS, 3 * EDGES), bf16)]
        + [pltpu.VMEM((9 * CH, EDGES), bf16)] * 2
        + [pltpu.VMEM((9 * CH, 3 * EDGES), bf16)],
        flops=40000000000,
    )(tl, tx, ty, geo, vcol, occ, first, second, third, *w["b2"], w["mf2"], w["mb2"], w["of2"],
      w["ob2"], w["coef2"], w["lin"], w["rh"], w["rht"], w["ro"])


def split_rows(x):
    hi = x.astype(bf16).astype(f32)
    rest = x - hi
    mid = rest.astype(bf16).astype(f32)
    return hi, mid, rest - mid


def place_border(x, border):
    slots = lax.broadcasted_iota(jnp.int32, (2 * LANES, LANES), 0)
    hot = (slots == border[...]).astype(f32).astype(bf16)
    n = x.shape[0]
    got = mm_nt(jnp.concatenate(split_rows(x), axis=0).astype(bf16), hot)
    return got[:n] + got[n : 2 * n] + got[2 * n :]


def columns_kernel(g2, g1, b0, b1, b2, b3, vcol, border, out, tot, lhs, hot):
    tot[...] = jnp.zeros_like(tot)
    for b in range(LOCAL):
        tot[b, 0:48, :] = g2[b] + g1[b]
    placed = place_border(b0[...] + b1[...] + (b2[...] + b3[...]), border)
    for b in range(2):
        tot[b, 0:48, :] = tot[b, 0:48, :] + placed[:, lanes(b)]
    iota = lax.broadcasted_iota(jnp.int32, (LANES, LANES), 0)
    total = jnp.zeros((16 * 11, LANES), f32)
    owns = []
    for b in range(LOCAL):
        own = jnp.zeros((4, LANES), f32)
        for s in range(SLOTS):
            x = tot[b, pl.ds(s, 4, stride=16), :]
            own = own + x
            hi, mid, lo = split_rows(x)
            part = jnp.concatenate([hi, mid, lo, jnp.zeros_like(x)], axis=0)
            v = vcol[b, s : s + 1, :]
            hot[:, lanes(s)] = (iota == (v & 127)).astype(f32).astype(bf16)
            block = v >> 7
            for k in range(11):
                lhs[k * 16 : k * 16 + 16, lanes(s)] = jnp.where(block == k, part, 0.0).astype(bf16)
        total = total + mm_nt(lhs[...], hot[...])
        owns.append(own)
    out[...] = jnp.zeros_like(out)
    for k in range(11):
        got = total[k * 16 : k * 16 + 4] + total[k * 16 + 4 : k * 16 + 8] + total[k * 16 + 8 : k * 16 + 12]
        out[0:4, lanes(k)] = got - owns[k] if k < LOCAL else got


def forces_kernel(col, r1, r2, xp, xn, border, out):
    total = xp[...] + xn[...] + (r1[:, lanes(1)] + r2[:, lanes(1)])
    placed = place_border(total, border)
    out[:, 0:256] = -(col[0:3, 0:256] + placed[0:3])
    out[:, 256:384] = -col[0:3, 256:384]


def from_behind(block, axis, distance):
    count = lax.axis_size(axis)
    route = [((i - distance) % count, i) for i in range(count)]
    return lax.ppermute(block, axis, route)


def eye(n):
    r = lax.broadcasted_iota(jnp.int32, (n, n), 0)
    return (r == lax.broadcasted_iota(jnp.int32, (n, n), 1)).astype(f32)


def turned(x):
    return lax.dot_general(
        eye(x.shape[1]), x, (((1,), (1,)), ((), ())), precision=lax.Precision.HIGHEST,
        preferred_element_type=f32,
    )


def left3(x):
    hi = x.astype(bf16).astype(f32)
    return jnp.concatenate([hi, hi, x - hi], axis=-1).astype(bf16)


def stacked(x):
    hi = x.astype(bf16).astype(f32)
    return jnp.concatenate([hi, x - hi], axis=0).astype(bf16)


def prepare_kernel(
    emb, rin, rmid, rout1, rout2, mix, mo1, mo2, c1, c2, lin, rh, ro,
    f1, s1, t1, f2, s2, t2, tt1, st1, ft1, tt2, st2, ft2, mf1, mb1, mf2, mb2, of1, ob1, of2, ob2,
    k1, k2, embo, lino, rho, rhto, roo, pad,
):
    for t, (f, s, o, tt, st, ft, out, mf, mb) in enumerate(
        ((f1, s1, t1, tt1, st1, ft1, rout1, mf1, mb1), (f2, s2, t2, tt2, st2, ft2, rout2, mf2, mb2))
    ):
        x = rin[t]
        hi = x.astype(bf16).astype(f32)
        top = turned(jnp.concatenate([hi, hi], axis=0))
        low = turned(jnp.concatenate([x - hi, jnp.zeros_like(x)], axis=0))
        f[...] = jnp.concatenate([top, low], axis=0).astype(bf16)
        s[...] = left3(turned(rmid[t]))
        for p in range(o.shape[0] // CH):
            o[p * CH : (p + 1) * CH, :] = left3(turned(out[:, lanes(p)]))
        tt[...] = stacked(out[...])
        st[...] = left3(rmid[t])
        ft[...] = left3(jnp.concatenate([x, jnp.zeros_like(x)], axis=0))
        for l in range(3):
            mf[l] = left3(turned(mix[t, l]))
            mb[l] = left3(mix[t, l])
    for l in range(3):
        of1[l] = left3(turned(mo1[l]))
        ob1[l] = left3(mo1[l])
    of2[...] = left3(turned(mo2[...]))
    ob2[...] = left3(mo2[...])
    k1[...] = turned(c1[...])
    k2[...] = turned(c2[...])
    pad[...] = jnp.zeros_like(pad)
    pad[0 : emb.shape[0], :] = emb[...]
    embo[...] = stacked(turned(pad[...]))
    lino[...] = turned(lin[...])
    rho[...] = left3(rh[...])
    rhto[...] = left3(turned(rh[...]))
    roo[...] = turned(ro[...])


def prepare(embedding, radial_in, radial_mid, outs, mix, mix_out_one, mix_out_two, product_one, product_two, read_lin, read_hidden, read_out):
    def half(*dims):
        return shape(*dims, kind=bf16)

    paths = [o.shape[1] for o in outs]
    small = lambda n: [half(128, 16), half(HID, 192), half(n, 192)]
    back = lambda n: [half(128, n), half(HID, 192), half(16, 192)]
    square = half(CH, 384)
    three = half(3, CH, 384)
    names = ("r1", "r2", "b1", "b2")
    shapes = small(paths[0]) + small(paths[1]) + back(paths[0]) + back(paths[1])
    shapes += [three] * 6 + [square] * 2
    shapes += [shape(CH, 5), shape(CH, 3), half(256, CH), shape(CH, 1), half(CH, 48), half(16, 384), shape(16, 1)]
    got = call(prepare_kernel, tuple(shapes), scratch=[pltpu.VMEM((CH, CH), f32)], flops=4000000000)(
        embedding, radial_in, radial_mid, *outs, mix, mix_out_one, mix_out_two, product_one,
        product_two, read_lin[None], read_hidden, read_out[None],
    )
    w = {n: tuple(got[3 * i : 3 * i + 3]) for i, n in enumerate(names)}
    rest = ("mf1", "mb1", "mf2", "mb2", "of1", "ob1", "of2", "ob2", "coef1", "coef2", "emb", "lin", "rh", "rht", "ro")
    w.update(zip(rest, got[12:]))
    return w


def on_device(
    positions, species, dest_key, send_list, send_count, border, neighbours, embedding, radial_in,
    radial_mid, radial_out_one, radial_out_two, mix, mix_out_one, mix_out_two, product_one,
    product_two, read_lin, read_hidden, read_out,
):
    pos = positions[0, 0]
    spec = species[0]
    key = dest_key[0]
    rows = border[0]
    nbr = neighbours[0, 0].T
    packet = call(
        packet_kernel,
        shape(8, 256),
        scratch=[pltpu.VMEM((8, 256), f32)],
        in_specs=[VMEM, VMEM, VMEM, VMEM, SMEM],
    )(pos, spec, send_list.reshape(1, LANES), rows, send_count.reshape(4))
    xp = from_behind(packet, "gx", 1)
    xn = from_behind(packet, "gx", -1)
    wide = jnp.concatenate([packet, xp[:, LANES:], xn[:, LANES:]], axis=1)
    yp = from_behind(wide, "gy", 1)
    yn = from_behind(wide, "gy", -1)
    w = prepare(embedding, radial_in, radial_mid, (radial_out_one, radial_out_two), mix, mix_out_one,
                mix_out_two, product_one, product_two, read_lin, read_hidden, read_out)
    geo, bgeo, vcol, kinds_l, kinds_x, kinds_y, occ = call(
        edges_kernel,
        (
            shape(LOCAL, 64, LANES),
            shape(64, LANES),
            shape(LOCAL, 16, LANES, kind=jnp.int32),
            shape(1, 384),
            shape(1, 256),
            shape(1, 768),
            shape(1, LOCAL * LANES),
        ),
        scratch=[pltpu.VMEM((8, COLS), f32)],
    )(pos, spec, key, xp, xn, yp, yn, nbr, rows)
    gxp = from_behind(bgeo, "gx", 1)
    gxn = from_behind(bgeo, "gx", -1)
    tl, kl = layer_one(geo, kinds_l, NL, w)
    three = jnp.stack([gxp, bgeo, gxn])
    gyp = from_behind(three, "gy", 1)
    gyn = from_behind(three, "gy", -1)
    geo_x = jnp.stack([gxp, gxn])
    tx, kx = layer_one(geo_x, kinds_x, NX, w)
    geo_y = jnp.concatenate([gyp, gyn], axis=0)
    ty, ky = layer_one(geo_y, kinds_y, NY, w)
    energy, dl, dx, dy, g2 = layer_two(tl, tx, ty, geo, vcol, occ, w)
    dgy = layer_one_back(geo_y, dy, ky, 1, w)
    ry1 = from_behind(dgy[0:3], "gy", -1)
    ry2 = from_behind(dgy[3:6], "gy", 1)
    dgx = layer_one_back(geo_x, dx, kx, 1, w)
    rx1 = from_behind(dgx[0] + ry1[0] + ry2[0], "gx", -1)
    rx2 = from_behind(dgx[1] + ry1[2] + ry2[2], "gx", 1)
    g1 = layer_one_back(geo, dl, kl, 1, w)
    col = call(
        columns_kernel,
        shape(8, COLS),
        scratch=[
            pltpu.VMEM((LOCAL, 64, LANES), f32),
            pltpu.VMEM((11 * 16, EDGES), bf16),
            pltpu.VMEM((LANES, EDGES), bf16),
        ],
    )(g2, g1, ry1[1], ry2[1], rx1, rx2, vcol, rows)
    r1 = from_behind(col[:, 640:1024], "gy", -1)
    r2 = from_behind(col[:, 1024:1408], "gy", 1)
    sx1 = from_behind(col[:, 384:512] + r1[:, 0:128] + r2[:, 0:128], "gx", -1)
    sx2 = from_behind(col[:, 512:640] + r1[:, 256:384] + r2[:, 256:384], "gx", 1)
    forces = call(forces_kernel, shape(3, LOCAL * LANES))(col, r1, r2, sx1, sx2, rows)
    return energy[None], forces[None, None]


def solution(mesh):
    along = P("gx", "gy")
    in_specs = (along,) * 7 + (P(),) * 13
    return jax.shard_map(
        on_device, mesh=mesh, in_specs=in_specs, out_specs=(along, along), check_vma=False
    )
```
